128 devices in a mesh: dp: 64 (over x, y_lo, z, core), tensor: 2 (over y_hi).
Axes of the slice: x: 4, y: 4 (y_hi: 2, y_lo: 2; y = y_hi * 2 + y_lo), z: 4, core: 2. Of those that a mesh axis runs over, the one named last changes fastest.
Arguments:
- tokens: bfloat16 [64, 512, 768], P('dp'), may hold values from -6 to 6
- seg_ids: int32 [64, 512], P('dp'), may hold values from 0 to 3, never falling along the last dimension, each value on 1 to 256 neighbouring positions
- pad_mask: int32 [64, 512], P('dp'), may hold values 0 or 1
- query_weight: bfloat16 [768, 768], P(None, 'tensor'), may hold values from -0.21875 to 0.21875
- query_bias: float32 [768], P('tensor'), may hold values from -1.75 to 1.75
- key_weight: bfloat16 [768, 768], P(None, 'tensor'), may hold values from -0.21875 to 0.21875
- value_weight: bfloat16 [768, 768], P(None, 'tensor'), may hold values from -0.21875 to 0.21875
- value_bias: float32 [768], P('tensor'), may hold values from -1.75 to 1.75
- out_weight: bfloat16 [768, 768], P('tensor'), may hold values from -1.75 to 1.75
- out_bias: float32 [768], replicated, may hold values from -1.75 to 1.75
- first_gain: float32 [768], replicated, may hold values from 0.25 to 1.75
- first_shift: float32 [768], replicated, may hold values from -1.75 to 1.75
- up_weight: bfloat16 [768, 3072], P(None, 'tensor'), may hold values from -0.21875 to 0.21875
- up_bias: float32 [3072], P('tensor'), may hold values from -1.75 to 1.75
- down_weight: bfloat16 [3072, 768], P('tensor'), may hold values from -0.109375 to 0.109375
- down_bias: float32 [768], replicated, may hold values from -1.75 to 1.75
- second_gain: float32 [768], replicated, may hold values from 0.25 to 1.75
- second_shift: float32 [768], replicated, may hold values from -1.75 to 1.75
- cotangent: bfloat16 [64, 512, 768], P('dp'), may hold values from -6 to 6
Outputs:
- mixed_out: bfloat16 [64, 512, 768], P('dp')
- input_gradient: float32 [64, 512, 768], P('dp')
- query_weight_gradient: float32 [768, 768], P(None, 'tensor')
- query_bias_gradient: float32 [768], P('tensor')
- key_weight_gradient: float32 [768, 768], P(None, 'tensor')
- value_weight_gradient: float32 [768, 768], P(None, 'tensor')
- value_bias_gradient: float32 [768], P('tensor')
- out_weight_gradient: float32 [768, 768], P('tensor')
- out_bias_gradient: float32 [768], replicated
- first_gain_gradient: float32 [768], replicated
- first_shift_gradient: float32 [768], replicated
- up_weight_gradient: float32 [768, 3072], P(None, 'tensor')
- up_bias_gradient: float32 [3072], P('tensor')
- down_weight_gradient: float32 [3072, 768], P('tensor')
- down_bias_gradient: float32 [768], replicated
- second_gain_gradient: float32 [768], replicated
- second_shift_gradient: float32 [768], replicated
The draws below stay inside these ranges and needn't reach their ends.
Inputs may be any that keep to these rules, and one draw needn't show every extreme that they name: `seg_ids`: ids never fall along a row; one document of each row holds exactly 256 tokens and none more.
All inputs are finite; a program needn't handle non-finite values. No bound on the sum of `pad_mask` on one device may be relied on, other than what follows from the above.
Results may differ from the reference program's by a relative error of at most 0.013.
The reference program's roundings to bfloat16 on the way count: a program that leaves them out, or rounds other values in their place, can miss the bound.
Values sent between devices are 32-bit elements; how exact they have to be, the bound alone decides.
No kernel may reach another device: no remote copies, remote signals or barrier semaphores. Data moves between devices by JAX's collectives and lax.ppermute only.
A program may use at most 128 MiB of HBM per device.

```python
import math
import jax
import jax.numpy as jnp
import numpy as np
from jax import lax

D = 768
HEAD_DIM = 64
FF = 3072
SEQ_LEN = 512
SEGS = 4
ROWS = 64


def touch_ends(values, own_key, smallest, top_value):
    place = [jax.random.randint(jax.random.fold_in(own_key, axis), (), 0, length) for axis, length in enumerate(values.shape)]
    longest = values.shape.index(max(values.shape))
    beside = place[:longest] + [(place[longest] + 1) % values.shape[longest]] + place[longest + 1:]
    return values.at[tuple(place)].set(smallest).at[tuple(beside)].set(top_value)


def block_levels(rng, extent, cuts, low, top_value):
    factor_of = 1.0
    for position, shards_of in cuts:
        draws = jax.random.uniform(jax.random.fold_in(jax.random.fold_in(rng, 6), position), (shards_of,), jnp.float32, low / len(cuts), top_value / len(cuts))
        factor_of = factor_of * jnp.repeat(jnp.exp(draws), extent[position] // shards_of).reshape((-1,) + (1,) * (len(extent) - 1 - position))
    return factor_of


def profile(amount, total, limit, slope):
    weights = [(1 << 20) // math.isqrt(rank ** slope) + 1 for rank in range(2, amount + 1)]
    rest, counts = total - limit - (amount - 1), [1] * (amount - 1)
    while rest > 0:
        candidates = [i for i in range(amount - 1) if counts[i] < limit]
        pool, remaining = sum([weights[i] for i in candidates]), rest
        for i in candidates:
            addition = min(limit - counts[i], max(1, remaining * weights[i] // pool), rest)
            counts[i] = counts[i] + addition
            rest = rest - addition
    return np.array([limit] + counts)


def ragged(own_key, count, total, bound, skew):
    if count == 2:
        one = jax.random.randint(own_key, (), max(1, total - bound), min(bound, total - 1) + 1)
        return jnp.stack([one, total - one])
    sizes = jnp.asarray(profile(count, total, bound, skew), jnp.int32)
    twos = (count - 1) // 2
    donor, taker = sizes[1:1 + 2 * twos:2], sizes[2:2 + 2 * twos:2]
    slack = jnp.minimum(donor - 1, bound - taker)
    passed = jax.random.randint(jax.random.fold_in(own_key, 1), (twos,), 0, 1 << 20) % (slack + 1)
    sizes = sizes.at[1:1 + 2 * twos:2].set(donor - passed).at[2:2 + 2 * twos:2].set(taker + passed)
    return sizes[jax.random.permutation(jax.random.fold_in(own_key, 2), count)]


def centred(own_key, shape, scale, limit, cuts=(), kind=jnp.bfloat16):
    values = scale * jax.random.normal(own_key, shape, jnp.float32)
    if cuts:
        values = values * block_levels(own_key, shape, cuts, -0.22, 0.18)
    return jnp.clip(values, -limit, limit).astype(kind)


def setup_inputs(seed: int = 0) -> dict:
    keys = jax.random.split(jax.random.key(seed), 20)
    return {
        "tokens": centred(keys[0], (ROWS, SEQ_LEN, D), 1.0, 6.0, ((0, 64),)),
        "seg_ids": jax.vmap(lambda own: jnp.searchsorted(jnp.cumsum(ragged(own, SEGS, SEQ_LEN, SEQ_LEN // 2, 1)), jnp.arange(SEQ_LEN), side="right"))(jax.random.split(keys[1], ROWS)).reshape((ROWS, SEQ_LEN)).astype(jnp.int32),
        "pad_mask": touch_ends((jax.random.randint(keys[2], (ROWS, SEQ_LEN), 0, 8) < 7).astype(jnp.int32), jax.random.fold_in(keys[2], 1), 0, 1),
        "query_weight": centred(keys[3], (D, D), D ** -0.5, 0.21875, ((1, 2),)),
        "query_bias": centred(keys[4], (D,), 0.3, 1.75, ((0, 2),), jnp.float32),
        "key_weight": centred(keys[5], (D, D), D ** -0.5, 0.21875, ((1, 2),)),
        "value_weight": centred(keys[6], (D, D), D ** -0.5, 0.21875, ((1, 2),)),
        "value_bias": centred(keys[7], (D,), 0.3, 1.75, ((0, 2),), jnp.float32),
        "out_weight": centred(keys[8], (D, D), (D * 8 // SEQ_LEN) ** -0.5, 1.75, ((0, 2),)),
        "out_bias": centred(keys[9], (D,), 0.3, 1.75, (), jnp.float32),
        "first_gain": jnp.clip(1.0 + 0.15 * jax.random.normal(keys[10], (D,), jnp.float32), 0.25, 1.75),
        "first_shift": centred(keys[11], (D,), 0.3, 1.75, (), jnp.float32),
        "up_weight": centred(keys[12], (D, FF), D ** -0.5, 0.21875, ((1, 2),)),
        "up_bias": centred(keys[13], (FF,), 0.3, 1.75, ((0, 2),), jnp.float32),
        "down_weight": centred(keys[14], (FF, D), FF ** -0.5, 0.109375, ((0, 2),)),
        "down_bias": centred(keys[15], (D,), 0.3, 1.75, (), jnp.float32),
        "second_gain": jnp.clip(1.0 + 0.15 * jax.random.normal(keys[16], (D,), jnp.float32), 0.25, 1.75),
        "second_shift": centred(keys[17], (D,), 0.3, 1.75, (), jnp.float32),
        "cotangent": centred(keys[18], (ROWS, SEQ_LEN, D), 1.0, 6.0, ((0, 64),)),
    }


EPSILON = 1e-06
NEG_LARGE = -1e+30

@jax.custom_vjp
def low(v):
    return lax.optimization_barrier(v.astype(jnp.bfloat16)).astype(jnp.float32)

@jax.custom_vjp
def low_back(v):
    return v

def low_keep(v):
    return (low(v), None)

def low_pass(kept, grad):
    return (grad,)

def back_keep(v):
    return (v, None)

def back_low(kept, grad):
    return (low(grad),)
low.defvjp(low_keep, low_pass)
low_back.defvjp(back_keep, back_low)

def product(left_op, right_op):
    return jnp.dot(left_op, right_op, precision=lax.Precision.HIGHEST)

def layer_norm(summed, gain_vec, shift_vec):
    center = summed - lax.optimization_barrier(jnp.mean(summed, axis=-1, keepdims=True))
    spread = lax.optimization_barrier(jnp.mean(center * center, axis=-1, keepdims=True))
    return center * lax.rsqrt(spread + EPSILON) * gain_vec + shift_vec

def attend_row(queries, keys_low, values_low, seg_row, pad_row):
    length = queries.shape[0]
    head_count = queries.shape[1] // HEAD_DIM
    query_heads = queries.reshape(length, head_count, HEAD_DIM)
    key_heads = keys_low.reshape(length, head_count, HEAD_DIM)
    value_heads = values_low.reshape(length, head_count, HEAD_DIM)
    raw_scores = jnp.einsum('qhd,khd->hqk', query_heads, key_heads, precision=lax.Precision.HIGHEST)
    scores = low_back(raw_scores * HEAD_DIM ** (-0.5))
    same_doc = seg_row[:, None] == seg_row[None, :]
    allowed = same_doc & (pad_row[None, :] == 1) | jnp.eye(length, dtype=bool)
    masked = jnp.where(allowed[None], scores, NEG_LARGE)
    row_peak = lax.optimization_barrier(jnp.max(masked, axis=-1, keepdims=True))
    exp_scores = jnp.exp(masked - row_peak)
    attention = low(exp_scores / lax.optimization_barrier(jnp.sum(exp_scores, axis=-1, keepdims=True)))
    mixed_heads = jnp.einsum('hqk,khd->qhd', attention, value_heads, precision=lax.Precision.HIGHEST)
    return mixed_heads.reshape(length, head_count * HEAD_DIM)

def forward(tokens, query_weight, query_bias, key_weight, value_weight, value_bias, out_weight, out_bias, first_gain, first_shift, up_weight, up_bias, down_weight, down_bias, second_gain, second_shift, seg_ids, pad_mask):
    group_rows, length, model_width = tokens.shape
    flat_tokens = tokens.reshape(group_rows * length, model_width)
    queries = low(low_back(product(flat_tokens, query_weight) + query_bias))
    keys_low = low(low_back(product(flat_tokens, key_weight)))
    values_low = low(low_back(product(flat_tokens, value_weight) + value_bias))

    def by_rows(matrix):
        return matrix.reshape(group_rows, length, matrix.shape[-1])

    def one_row(pieces):
        return jax.checkpoint(attend_row)(*pieces)
    attended = lax.map(one_row, (by_rows(queries), by_rows(keys_low), by_rows(values_low), seg_ids, pad_mask))
    attended = low(low_back(attended.reshape(group_rows * length, -1)))
    attention_out = low_back(product(attended, out_weight))
    hidden_state = layer_norm(flat_tokens + attention_out + out_bias, first_gain, first_shift)
    up_value = low_back(product(low(hidden_state), up_weight) + up_bias)
    activation = low(jax.nn.gelu(up_value, approximate=False))
    feed_out = low_back(product(activation, down_weight))
    result = layer_norm(hidden_state + feed_out + down_bias, second_gain, second_shift)
    return result.reshape(group_rows, length, model_width)

def reference(tokens, seg_ids, pad_mask, query_weight, query_bias, key_weight, value_weight, value_bias, out_weight, out_bias, first_gain, first_shift, up_weight, up_bias, down_weight, down_bias, second_gain, second_shift, cotangent):
    total_rows, length, model_width = tokens.shape
    group_rows = math.gcd(total_rows, max(1, 4096 // length))
    blocks = total_rows // group_rows
    params = tuple((weight.astype(jnp.float32) for weight in (query_weight, query_bias, key_weight, value_weight, value_bias, out_weight, out_bias, first_gain, first_shift, up_weight, up_bias, down_weight, down_bias, second_gain, second_shift)))
    token_blocks = tokens.astype(jnp.float32).reshape(blocks, group_rows, length, model_width)
    cot_blocks = cotangent.astype(jnp.float32).reshape(blocks, group_rows, length, model_width)
    seg_blocks = seg_ids.reshape(blocks, group_rows, length)
    pad_blocks = pad_mask.reshape(blocks, group_rows, length)

    def step_fn(totals, block_item):
        tok_block, seg_block, pad_block, cot_block = block_item

        def local_forward(tok_arg, *weights):
            return forward(tok_arg, *weights, seg_block, pad_block)
        output, pullback = jax.vjp(local_forward, tok_block, *params)
        gradients = pullback(cot_block)
        totals = tuple((running + fresh for running, fresh in zip(totals, gradients[1:])))
        return (totals, (output.astype(jnp.bfloat16), gradients[0]))
    zeros_init = tuple((jnp.zeros(weight.shape, jnp.float32) for weight in params))
    totals, (outputs, input_grads) = lax.scan(step_fn, zeros_init, (token_blocks, seg_blocks, pad_blocks, cot_blocks))
    mixed_out = outputs.reshape(total_rows, length, model_width)
    input_gradient = input_grads.reshape(total_rows, length, model_width)
    return (mixed_out, input_gradient, totals[0], totals[1], totals[2], totals[3], totals[4], totals[5], totals[6], totals[7], totals[8], totals[9], totals[10], totals[11], totals[12], totals[13], totals[14])
```

```python
import jax
import jax.numpy as jnp
from jax import lax
from jax.experimental import pallas as pl
from jax.experimental.pallas import tpu as pltpu
from jax.sharding import PartitionSpec as P

HEAD_DIM = 64


EPSILON = 1e-06
NEG_LARGE = -1e30


def layer_norm(summed, gain_vec, shift_vec):
    center = summed - jnp.mean(summed, axis=-1, keepdims=True)
    spread = jnp.mean(center * center, axis=-1, keepdims=True)
    return center * lax.rsqrt(spread + EPSILON) * gain_vec + shift_vec


def gelu_exact(up_value):
    return jax.nn.gelu(up_value, approximate=False)


def contract_rows(left_op, right_op):
    return lax.dot_general(
        left_op, right_op, (((0,), (0,)), ((), ())), preferred_element_type=jnp.float32
    )


def times_transposed(left_op, right_op):
    return lax.dot_general(
        left_op, right_op, (((1,), (1,)), ((), ())), preferred_element_type=jnp.float32
    )


def allowed_of(seg_row, pad_row):
    length = seg_row.shape[0]
    same_doc = seg_row[:, None] == seg_row[None, :]
    diagonal = lax.broadcasted_iota(jnp.int32, (length, length), 0) == lax.broadcasted_iota(
        jnp.int32, (length, length), 1
    )
    return same_doc & (pad_row[None, :] == 1) | diagonal


def masked_scores(query_heads, key_heads, allowed):
    raw_scores = jnp.einsum(
        "qhd,khd->hqk", query_heads, key_heads, preferred_element_type=jnp.float32
    )
    return jnp.where(allowed[None], raw_scores * HEAD_DIM ** (-0.5), NEG_LARGE)


def attend_row(pieces):
    query_heads, key_heads, value_heads, allowed = pieces
    scores = masked_scores(query_heads, key_heads, allowed)
    row_peak = jnp.max(scores, axis=-1, keepdims=True)
    exp_scores = jnp.exp(scores - row_peak)
    row_total = jnp.sum(exp_scores, axis=-1, keepdims=True)
    attention = (exp_scores / row_total).astype(jnp.bfloat16)
    mixed_heads = jnp.einsum(
        "hqk,khd->qhd", attention, value_heads, preferred_element_type=jnp.float32
    )
    return (mixed_heads.astype(jnp.bfloat16), (row_peak + jnp.log(row_total))[..., 0])


def attend_back(pieces):
    query_heads, key_heads, value_heads, allowed, log_total, grad_heads = pieces
    scores = masked_scores(query_heads, key_heads, allowed)
    attention = jnp.exp(scores - log_total[..., None])
    value_grad = jnp.einsum(
        "hqk,qhd->khd",
        attention.astype(jnp.bfloat16),
        grad_heads,
        preferred_element_type=jnp.float32,
    )
    softmax_grad = jnp.einsum(
        "qhd,khd->hqk", grad_heads, value_heads, preferred_element_type=jnp.float32
    )
    row_inner = jnp.sum(softmax_grad * attention, axis=-1, keepdims=True)
    score_grad = (attention * (softmax_grad - row_inner)).astype(jnp.bfloat16)
    score_scale = HEAD_DIM ** (-0.5)
    query_grad = (
        jnp.einsum("hqk,khd->qhd", score_grad, key_heads, preferred_element_type=jnp.float32)
        * score_scale
    )
    key_grad = (
        jnp.einsum("hqk,qhd->khd", score_grad, query_heads, preferred_element_type=jnp.float32)
        * score_scale
    )
    return (
        query_grad.astype(jnp.bfloat16),
        key_grad.astype(jnp.bfloat16),
        value_grad.astype(jnp.bfloat16),
    )


def ring(axis, shift):
    count = 2 if axis in ("w", "c", "t") else 4
    return [(i, (i + shift) % count) for i in range(count)]


def send(value, axis, shift):
    return lax.ppermute(value, axis, ring(axis, shift))


def pick(stack, index):
    return lax.dynamic_index_in_dim(stack, index, 0, keepdims=False)


def rotated(stack, first):
    return [pick(stack, (first + j) % 4) for j in range(4)]


def placed(parts, first):
    out = jnp.zeros((4,) + parts[0].shape, parts[0].dtype)
    for j in range(4):
        out = lax.dynamic_update_index_in_dim(out, parts[j], (first + j) % 4, 0)
    return out


def reduce_relay(parts, axis):
    far = parts[2]
    half = far.shape[0] // 2
    from_left = send(far[:half], axis, 1)
    from_right = send(far[half:], axis, -1)
    right = jnp.concatenate([parts[1][:half] + from_left, parts[1][half:]], 0)
    left = jnp.concatenate([parts[3][:half], parts[3][half:] + from_right], 0)
    return parts[0] + send(right, axis, 1) + send(left, axis, -1)


def reduce_direct(parts, axis):
    return (parts[0] + send(parts[1], axis, 1)) + (send(parts[2], axis, 2) + send(parts[3], axis, -1))


def gather_relay(part, axis):
    half = part.shape[0] // 2
    right = send(part, axis, -1)
    left = send(part, axis, 1)
    far_top = send(left[:half], axis, 1)
    far_low = send(right[half:], axis, -1)
    return [part, right, jnp.concatenate([far_top, far_low], 0), left]


def gather_direct(part, axis):
    return [part, send(part, axis, -1), send(part, axis, 2), send(part, axis, 1)]


def sum_rows(group, big, small):
    core = lax.axis_index("c")
    mine = pick(group, core) + send(pick(group, 1 - core), "c", 1)
    parts = rotated(mine, lax.axis_index(big))
    strip = reduce_relay([p.reshape(-1, p.shape[-1]) for p in parts], big).reshape(parts[0].shape)
    piece = reduce_direct(rotated(strip, lax.axis_index(small)), small)
    return piece + send(piece, "w", 1)


def spread_rows(piece, big, small):
    core = lax.axis_index("c")
    strip = placed(gather_direct(piece, small), lax.axis_index(small))
    flat = strip.reshape(-1, strip.shape[-1])
    mine = placed(gather_relay(flat, big), lax.axis_index(big)).reshape((4,) + strip.shape)
    other = send(mine, "c", 1)
    both = jnp.stack([mine, other])
    return jnp.stack([pick(both, core), pick(both, 1 - core)])


def low_kernel(core_ref, mine_ref, other_ref, first_ref, second_ref):
    core = core_ref[0]

    @pl.when(core == 0)
    def _():
        first_ref[...] = mine_ref[...].astype(jnp.bfloat16)
        second_ref[...] = other_ref[...].astype(jnp.bfloat16)

    @pl.when(core == 1)
    def _():
        first_ref[...] = other_ref[...].astype(jnp.bfloat16)
        second_ref[...] = mine_ref[...].astype(jnp.bfloat16)


def to_low(mine, other, core):
    shape = jax.ShapeDtypeStruct(mine.shape, jnp.bfloat16)
    vmem = pl.BlockSpec(memory_space=pltpu.VMEM)
    return pl.pallas_call(
        low_kernel,
        out_shape=(shape, shape),
        in_specs=[pl.BlockSpec(memory_space=pltpu.SMEM), vmem, vmem],
        out_specs=(vmem, vmem),
        compiler_params=pltpu.CompilerParams(vmem_limit_bytes=32 << 20),
    )(core.reshape(1), mine, other)


def fetch_rows(shard, first, second):
    core = lax.axis_index("c")
    strip = placed(gather_direct(shard, first), lax.axis_index(first))
    flat = strip.reshape(-1, strip.shape[-1])
    mine = placed(gather_relay(flat, second), lax.axis_index(second))
    mine = mine.reshape(-1, mine.shape[-1])
    return to_low(mine, send(mine, "c", 1), core)


CROSS = [(0, 3), (3, 0), (1, 2), (2, 1)]


def on_device(
    tokens,
    seg_ids,
    pad_mask,
    query_weight,
    query_bias,
    key_weight,
    value_weight,
    value_bias,
    out_weight,
    out_bias,
    first_gain,
    first_shift,
    up_weight,
    up_bias,
    down_weight,
    down_bias,
    second_gain,
    second_shift,
    cotangent,
):
    seq_count, length, model_width = tokens.shape
    local_width = query_weight.shape[1]
    head_count = local_width // HEAD_DIM
    flat_tokens = tokens.reshape(seq_count * length, model_width)
    at_x, at_z, at_c = (lax.axis_index(name) for name in ("x", "z", "c"))

    up_shard = lax.dynamic_slice(up_weight, ((at_z * 4 + at_x) * 48, at_c * 768), (48, 768))
    down_shard = lax.dynamic_slice(down_weight, (at_c * 768 + (at_x * 4 + at_z) * 48, 0), (48, 768))
    shards = jnp.concatenate([up_shard, down_shard], 0).astype(jnp.float32)
    shards = lax.ppermute(shards, ("w", "t"), CROSS)
    up_other = jnp.concatenate(fetch_rows(shards[:48], "x", "z"), 1)
    down_other = jnp.concatenate(fetch_rows(shards[48:], "z", "x"), 0)
    up_bias_other = send(up_bias, "t", 1)

    def to_heads(matrix):
        return matrix.reshape(seq_count, length, head_count, HEAD_DIM)

    def to_flat(stacked):
        return stacked.reshape(seq_count * length, local_width)

    queries = (
        jnp.dot(flat_tokens, query_weight, preferred_element_type=jnp.float32) + query_bias
    ).astype(jnp.bfloat16)
    keys_low = jnp.dot(flat_tokens, key_weight, preferred_element_type=jnp.float32).astype(
        jnp.bfloat16
    )
    values_low = (
        jnp.dot(flat_tokens, value_weight, preferred_element_type=jnp.float32) + value_bias
    ).astype(jnp.bfloat16)
    allowed = jax.vmap(allowed_of)(seg_ids, pad_mask)
    attended, log_total = lax.map(
        attend_row, (to_heads(queries), to_heads(keys_low), to_heads(values_low), allowed)
    )
    attended = to_flat(attended)
    attention_part = jnp.dot(attended, out_weight, preferred_element_type=jnp.float32)
    attention_out = attention_part + send(attention_part, "t", 1)
    first_in = flat_tokens.astype(jnp.float32) + attention_out + out_bias
    hidden_state, first_pull = jax.vjp(layer_norm, first_in, first_gain, first_shift)
    hidden_low = hidden_state.astype(jnp.bfloat16)

    def feed(up_half, bias_half, down_half):
        up_value = jnp.dot(hidden_low, up_half, preferred_element_type=jnp.float32) + bias_half
        gelu_value, gelu_pull = jax.vjp(gelu_exact, up_value)
        activation = gelu_value.astype(jnp.bfloat16)
        return activation, gelu_pull, jnp.dot(activation, down_half, preferred_element_type=jnp.float32)

    activation, gelu_pull, feed_own = feed(up_weight, up_bias, down_weight)
    _, gelu_pull_other, feed_other = feed(up_other, up_bias_other, down_other)
    second_in = hidden_state + (feed_own + feed_other) + down_bias
    output, second_pull = jax.vjp(layer_norm, second_in, second_gain, second_shift)
    mixed_out = output.astype(jnp.bfloat16).reshape(seq_count, length, model_width)
    out_grad = cotangent.astype(jnp.float32).reshape(seq_count * length, model_width)
    second_grad, second_gain_grad, second_shift_grad = second_pull(out_grad)
    down_bias_grad = jnp.sum(second_grad, axis=0)
    second_low = second_grad.astype(jnp.bfloat16)
    down_weight_grad = contract_rows(activation, second_low)
    down_piece = sum_rows(down_weight_grad.reshape(2, 4, 4, 48, 768), "x", "z")

    def feed_back(pull, up_half, down_half):
        activation_grad = times_transposed(second_low, down_half)
        up_grad = pull(activation_grad)[0].astype(jnp.bfloat16)
        return up_grad, times_transposed(up_grad, up_half)

    up_grad, entry_own = feed_back(gelu_pull, up_weight, down_weight)
    _, entry_other = feed_back(gelu_pull_other, up_other, down_other)
    up_weight_grad = contract_rows(hidden_low, up_grad)
    up_piece = sum_rows(
        up_weight_grad.reshape(768, 2, 768).transpose(1, 0, 2).reshape(2, 4, 4, 48, 768), "z", "x"
    )
    up_bias_grad = jnp.sum(up_grad.astype(jnp.float32), axis=0)
    hidden_grad = second_grad + (entry_own + entry_other)
    first_grad, first_gain_grad, first_shift_grad = first_pull(hidden_grad)
    out_bias_grad = jnp.sum(first_grad, axis=0)
    first_low = first_grad.astype(jnp.bfloat16)
    out_weight_grad = contract_rows(attended, first_low)
    attended_grad = times_transposed(first_low, out_weight).astype(jnp.bfloat16)
    query_grad, key_grad, value_grad = lax.map(
        attend_back,
        (
            to_heads(queries),
            to_heads(keys_low),
            to_heads(values_low),
            allowed,
            log_total,
            to_heads(attended_grad),
        ),
    )
    query_grad = to_flat(query_grad)
    key_grad = to_flat(key_grad)
    value_grad = to_flat(value_grad)
    query_weight_grad = contract_rows(flat_tokens, query_grad)
    query_bias_grad = jnp.sum(query_grad.astype(jnp.float32), axis=0)
    key_weight_grad = contract_rows(flat_tokens, key_grad)
    value_weight_grad = contract_rows(flat_tokens, value_grad)
    value_bias_grad = jnp.sum(value_grad.astype(jnp.float32), axis=0)
    entry_part = (
        times_transposed(query_grad, query_weight)
        + times_transposed(key_grad, key_weight)
        + times_transposed(value_grad, value_weight)
    )
    input_gradient = first_grad + (entry_part + send(entry_part, "t", 1))
    input_gradient = input_gradient.reshape(seq_count, length, model_width)

    vectors = jnp.concatenate(
        [
            query_bias_grad,
            value_bias_grad,
            out_bias_grad,
            first_gain_grad,
            first_shift_grad,
            up_bias_grad,
            down_bias_grad,
            second_gain_grad,
            second_shift_grad,
        ]
    ).reshape(9, 768)
    left = jnp.concatenate([query_weight_grad, key_weight_grad], 1)
    right = jnp.concatenate(
        [value_weight_grad, jnp.concatenate([out_weight_grad[:, :384], out_weight_grad[:, 384:]], 0)], 1
    )
    sides = jnp.stack([left, right]).reshape(2, 4, 4, 48, 768)
    extra = jnp.zeros((256, 768), jnp.float32).at[:9].set(vectors).reshape(2, 4, 4, 8, 768)
    side_piece = sum_rows(jnp.concatenate([sides, extra], 3), "x", "z")

    down_sum = spread_rows(down_piece, "x", "z").reshape(1536, 768)
    up_sum = spread_rows(up_piece, "z", "x").reshape(2, 768, 768).transpose(1, 0, 2).reshape(768, 1536)
    side_sum = spread_rows(side_piece, "x", "z")
    left, right = side_sum[:, :, :, :48].reshape(2, 768, 768)
    vector_sum = side_sum[:, :, :, 48:].reshape(256, 768)[:9].reshape(-1)
    out_sum = jnp.concatenate([right[:384, 384:], right[384:, 384:]], 1)
    cuts = [384, 768, 1536, 2304, 3072, 4608, 5376, 6144]
    qb, vb, ob, fg, fs, ub, db, sg, ss = jnp.split(vector_sum, cuts)
    return (
        mixed_out,
        input_gradient,
        left[:, :384],
        qb,
        left[:, 384:],
        right[:, :384],
        vb,
        out_sum,
        ob,
        fg,
        fs,
        up_sum,
        ub,
        down_sum,
        db,
        sg,
        ss,
    )


ROWS_AXES = ("x", "w", "z", "c")


def solution(mesh):
    fine = jax.sharding.Mesh(mesh.devices.reshape(4, 2, 4, 2, 2), ROWS_AXES + ("t",))
    by_row = P(ROWS_AXES, None, None)
    return jax.shard_map(
        on_device,
        mesh=fine,
        in_specs=(
            by_row,
            P(ROWS_AXES, None),
            P(ROWS_AXES, None),
            P(None, "t"),
            P("t"),
            P(None, "t"),
            P(None, "t"),
            P("t"),
            P("t", None),
            P(),
            P(),
            P(),
            P(None, "t"),
            P("t"),
            P("t", None),
            P(),
            P(),
            P(),
            by_row,
        ),
        out_specs=(
            by_row,
            by_row,
            P(None, "t"),
            P("t"),
            P(None, "t"),
            P(None, "t"),
            P("t"),
            P("t", None),
            P(),
            P(),
            P(),
            P(None, "t"),
            P("t"),
            P("t", None),
            P(),
            P(),
            P(),
        ),
        check_vma=False,
    )
```

```python
import math

import jax
import jax.numpy as jnp
from jax import lax
from jax.experimental import pallas as pl
from jax.experimental.pallas import tpu as pltpu
from jax.sharding import PartitionSpec as P

EPSILON = 1e-06
NEG_LARGE = -1e30
LOW = jnp.bfloat16
F32 = jnp.float32
LEN = 512
DIM = 768
HALF = 384
HEADS = 6
STEP = 32
PIECE = 48
VMEM = pl.BlockSpec(memory_space=pltpu.VMEM)
SMEM = pl.BlockSpec(memory_space=pltpu.SMEM)
ANY = pl.BlockSpec(memory_space=pl.ANY)


def nn(left_op, right_op):
    return jnp.dot(left_op, right_op, preferred_element_type=F32)


def nt(left_op, right_op):
    return lax.dot_general(left_op, right_op, (((1,), (1,)), ((), ())), preferred_element_type=F32)


def tn(left_op, right_op):
    return lax.dot_general(left_op, right_op, (((0,), (0,)), ((), ())), preferred_element_type=F32)


def shaped(*shape, kind=F32):
    return jax.ShapeDtypeStruct(shape, kind)


def run(kernel, outs, place, args, scratch=(), cost=2e9, spare=8):
    in_specs = [VMEM] * len(args)
    if place is not None:
        args = (place,) + tuple(args)
        in_specs = [SMEM] + in_specs
    need = sum(math.prod(s.shape) * jnp.dtype(s.dtype).itemsize for s in scratch)
    return pl.pallas_call(
        kernel,
        out_shape=outs,
        in_specs=in_specs,
        out_specs=jax.tree.map(lambda _: VMEM, outs),
        scratch_shapes=scratch,
        name=kernel.__name__,
        compiler_params=pltpu.CompilerParams(vmem_limit_bytes=need + (spare << 20)),
        cost_estimate=pl.CostEstimate(flops=int(cost), bytes_accessed=1 << 20, transcendentals=0),
    )(*args)


def over_rows(body, count=LEN // STEP, unroll=LEN // STEP):
    def step(i, carry):
        body(pl.ds(pl.multiple_of(i * STEP, STEP), STEP), i)
        return carry

    lax.fori_loop(0, count, step, 0, unroll=unroll)


def fold(values):
    return jnp.sum(values.reshape(STEP // 8, 8, values.shape[-1]), axis=0)


def fill_bias(seg_col, seg_row, pad_row, bias):
    def body(rows, i):
        down = lax.broadcasted_iota(jnp.int32, (STEP, LEN), 0) + i * STEP
        across = lax.broadcasted_iota(jnp.int32, (STEP, LEN), 1)
        same = (seg_col[rows, :] == seg_row[...]) & (pad_row[...] == 1)
        bias[rows, :] = jnp.where(same | (down == across), 0.0, NEG_LARGE)

    over_rows(body)


def head_of(pair, head):
    lane = lax.broadcasted_iota(jnp.int32, pair.shape, 1)
    return jnp.where((lane < 64) == (head == 0), pair.astype(F32), 0.0)


def attend_kernel(
    seg_col, seg_row, pad_row, tok, wq, wk, wv, qb, vb, wo, ub, q_ref, k_ref, v_ref, att_ref, lse_ref, part_ref, bias, s_scr, p_scr
):
    tokens = tok[...]
    q_ref[...] = (nn(tokens, wq[...]) + qb[...]).astype(LOW)
    k_ref[...] = nn(tokens, wk[...]).astype(LOW)
    v_ref[...] = (nn(tokens, wv[...]) + vb[...]).astype(LOW)
    fill_bias(seg_col, seg_row, pad_row, bias)
    for pair in range(HEADS // 2):
        cols = slice(pair * 128, pair * 128 + 128)
        outs = []
        for head in range(2):
            s_scr[...] = nt((head_of(q_ref[:, cols], head) * 0.125).astype(LOW), k_ref[:, cols])
            column = 2 * pair + head

            def body(rows, i, column=column):
                scores = s_scr[rows, :] + bias[rows, :]
                peak = jnp.max(scores, axis=-1, keepdims=True)
                grown = jnp.exp(scores - peak)
                total = jnp.sum(grown, axis=-1, keepdims=True)
                p_scr[rows, :] = (grown * (1.0 / total)).astype(LOW)
                lse_ref[rows, column : column + 1] = peak + jnp.log(total)

            over_rows(body)
            outs.append(nn(p_scr[...], v_ref[:, cols]))
        lane = lax.broadcasted_iota(jnp.int32, outs[0].shape, 1)
        att_ref[:, cols] = jnp.where(lane < 64, outs[0], outs[1]).astype(LOW)
    part_ref[:LEN, :] = nn(att_ref[...], wo[...])
    part_ref[LEN:, :] = ub[...]


def place_pieces(dst, pieces, big, small):
    own, right, left, far_top, far_low = pieces
    for turn, source, start, count in ((0, own, 0, 4), (1, right, 0, 4), (3, left, 0, 4), (2, far_top, 0, 2), (2, far_low, 2, 2)):
        for j in range(count):
            row = ((big + turn) & 3) * (4 * PIECE) + ((small + start + j) & 3) * PIECE
            dst[pl.ds(pl.multiple_of(row, PIECE), PIECE), :] = source[j * PIECE : (j + 1) * PIECE, :].astype(LOW)


def up_kernel(
    place, mine, theirs, tok, ob, g1, s1, wup, ub, *rest
):
    pieces, rest = rest[:10], rest[10:]
    low_ref, zhat_ref, r_ref, act_own, act_oth, dg_own, dg_oth, wup_oth, u_scr = rest
    core, big, small = place[0], place[1], place[2]
    place_pieces(wup_oth.at[core], pieces[:5], big, small)
    place_pieces(wup_oth.at[1 - core], pieces[5:], big, small)

    def norm(rows, i):
        z = tok[rows, :].astype(F32) + (mine[rows, :] + theirs[rows, :]) + ob[...]
        center = z - jnp.mean(z, axis=-1, keepdims=True)
        r = lax.rsqrt(jnp.mean(center * center, axis=-1, keepdims=True) + EPSILON)
        zhat = center * r
        zhat_ref[rows, :] = zhat
        r_ref[rows, :] = r
        low_ref[rows, :] = (zhat * g1[...] + s1[...]).astype(LOW)

    over_rows(norm)
    for side in range(2):
        for half in range(2):
            for chunk in range(3):
                cols = slice(chunk * 256, chunk * 256 + 256)
                wide = slice(half * DIM + chunk * 256, half * DIM + chunk * 256 + 256)
                if side == 0:
                    weight, bias, act, dg = wup[:, wide], ub[half : half + 1, cols], act_own, dg_own
                else:
                    weight, bias, act, dg = wup_oth[half, :, cols], theirs[LEN + half : LEN + half + 1, cols], act_oth, dg_oth
                u_scr[...] = nn(low_ref[...], weight) + bias

                def gelu(rows, i, act=act, dg=dg, wide=wide):
                    u = u_scr[rows, :]
                    cdf = 0.5 + 0.5 * lax.erf(u * (0.5**0.5))
                    act[rows, wide] = (u * cdf).astype(LOW)
                    dg[rows, wide] = cdf + u * (jnp.exp(-0.5 * (u * u)) * 0.3989422804014327)

                over_rows(gelu)


def down_kernel(
    place, zhat1, g1, s1, act_own, act_oth, wdown, db, g2, s2, cot, *rest
):
    pieces, rest = rest[:10], rest[10:]
    mixed_ref, sgrad_ref, slow_ref, vec_ref, wdown_oth, own_scr, oth_scr, acc = rest
    core, big, small = place[0], place[1], place[2]
    place_pieces(wdown_oth.at[core], pieces[:5], big, small)
    place_pieces(wdown_oth.at[1 - core], pieces[5:], big, small)
    own_scr[...] = nn(act_own[:, :DIM], wdown[:DIM, :])
    own_scr[...] += nn(act_own[:, DIM:], wdown[DIM:, :])
    oth_scr[...] = nn(act_oth[:, :DIM], wdown_oth[0])
    oth_scr[...] += nn(act_oth[:, DIM:], wdown_oth[1])
    acc[...] = jnp.zeros_like(acc)

    def body(rows, i):
        hidden = zhat1[rows, :] * g1[...] + s1[...]
        z = hidden + (own_scr[rows, :] + oth_scr[rows, :]) + db[...]
        center = z - jnp.mean(z, axis=-1, keepdims=True)
        r = lax.rsqrt(jnp.mean(center * center, axis=-1, keepdims=True) + EPSILON)
        zhat = center * r
        mixed_ref[rows, :] = (zhat * g2[...] + s2[...]).astype(LOW)
        g = cot[rows, :].astype(F32)
        u = g * g2[...]
        grad = r * (u - jnp.mean(u, axis=-1, keepdims=True) - zhat * jnp.mean(u * zhat, axis=-1, keepdims=True))
        sgrad_ref[rows, :] = grad
        slow_ref[rows, :] = grad.astype(LOW)
        acc[0] += fold(grad)
        acc[1] += fold(g * zhat)
        acc[2] += fold(g)

    over_rows(body)
    put_sums(vec_ref, acc, 3)


def put_sums(vec_ref, acc, count):
    vec_ref[...] = jnp.zeros_like(vec_ref)
    for k in range(count):
        vec_ref[k : k + 1, :] = jnp.sum(acc[k], axis=0, keepdims=True)


def put_turned(sums, keep, send, core, big, small, rows, extra=None):
    for j in range(4):
        for k in range(4):
            at_big, at_small = (big + j) & 3, (small + k) & 3
            source = pl.ds(pl.multiple_of(at_big * (4 * PIECE) + at_small * PIECE, PIECE), PIECE)
            start = (4 * j + k) * rows
            keep[start : start + PIECE, :] = sums[core, source, :]
            send[start : start + PIECE, :] = sums[1 - core, source, :]
            if extra is not None:
                first = (at_big + at_small) == 0
                keep[start + PIECE : start + rows, :] = jnp.where(first, extra[core], 0.0)
                send[start + PIECE : start + rows, :] = jnp.where(first, extra[1 - core], 0.0)


def down_grad_kernel(place, act_own, slow, keep, send, sums):
    sums[0] = tn(act_own[:, :DIM], slow[...])
    sums[1] = tn(act_own[:, DIM:], slow[...])
    put_turned(sums, keep, send, place[0], place[1], place[2], PIECE)


def up_grad_kernel(place, slow, wdown, dg_own, low, ug_ref, vec_ref, keep, send, sums, a_scr, acc):
    acc[...] = jnp.zeros_like(acc)
    for half in range(2):
        wide = slice(half * DIM, half * DIM + DIM)
        a_scr[...] = nt(slow[...], wdown[wide, :])

        def body(rows, i, half=half, wide=wide):
            grad = (a_scr[rows, :] * dg_own[rows, wide]).astype(LOW)
            ug_ref[rows, wide] = grad
            acc[half] += fold(grad.astype(F32))

        over_rows(body)
        sums[half] = tn(low[...], ug_ref[:, wide])
    put_sums(vec_ref, acc, 2)
    put_turned(sums, keep, send, place[0], place[1], place[2], PIECE)


def entry_kernel(
    slow, wdown_oth, dg_oth, wup, wup_oth, ug_own, sgrad, zhat1, r1, g1, att, wo, first_ref, attg_ref, gwo_ref, vec_ref, a_scr, ug_scr, own_scr, oth_scr, low_scr, acc
):
    acc[...] = jnp.zeros_like(acc)
    own_scr[...] = nt(ug_own[:, :DIM], wup[:, :DIM])
    own_scr[...] += nt(ug_own[:, DIM:], wup[:, DIM:])
    for half in range(2):
        wide = slice(half * DIM, half * DIM + DIM)
        a_scr[...] = nt(slow[...], wdown_oth[half])

        def body(rows, i, wide=wide):
            ug_scr[rows, :] = (a_scr[rows, :] * dg_oth[rows, wide]).astype(LOW)

        over_rows(body)
        if half == 0:
            oth_scr[...] = nt(ug_scr[...], wup_oth[half])
        else:
            oth_scr[...] += nt(ug_scr[...], wup_oth[half])

    def norm(rows, i):
        g = sgrad[rows, :] + (own_scr[rows, :] + oth_scr[rows, :])
        zhat = zhat1[rows, :]
        u = g * g1[...]
        grad = r1[rows, :] * (u - jnp.mean(u, axis=-1, keepdims=True) - zhat * jnp.mean(u * zhat, axis=-1, keepdims=True))
        first_ref[rows, :] = grad
        low_scr[rows, :] = grad.astype(LOW)
        acc[0] += fold(grad)
        acc[1] += fold(g * zhat)
        acc[2] += fold(g)

    over_rows(norm)
    put_sums(vec_ref, acc, 3)
    attg_ref[...] = nt(low_scr[...], wo[...]).astype(LOW)
    gwo_ref[...] = tn(att[...], low_scr[...])


def attend_back_kernel(
    place, seg_col, seg_row, pad_row, q, k, v, attg, lse, tok, gwo, vec1, vec2, vec3, dq_ref, dk_ref, dv_ref, keep, send,
    bias, s_scr, g_scr, p_scr, d_scr, dk_scr, dv_scr, sums, extra,
):
    fill_bias(seg_col, seg_row, pad_row, bias)
    for pair in range(HEADS // 2):
        cols = slice(pair * 128, pair * 128 + 128)
        q_turned = q[:, cols].T
        g_turned = attg[:, cols].T
        outs = []
        for head in range(2):
            s_scr[...] = nt((head_of(q[:, cols], head) * 0.125).astype(LOW), k[:, cols])
            g_scr[...] = nt(head_of(attg[:, cols], head).astype(LOW), v[:, cols])
            column = 2 * pair + head

            def body(rows, i, column=column):
                attention = jnp.exp(s_scr[rows, :] + bias[rows, :] - lse[rows, column : column + 1])
                grad = g_scr[rows, :]
                p_scr[rows, :] = attention.astype(LOW)
                inner = jnp.sum(grad * attention, axis=-1, keepdims=True)
                d_scr[rows, :] = (attention * (grad - inner)).astype(LOW)

            over_rows(body)
            rows = slice(64 * column, 64 * column + 64)
            mine = slice(64 * head, 64 * head + 64)
            outs.append(nn(d_scr[...], k[:, cols]))
            dk_scr[rows, :] = nn(q_turned[mine, :], d_scr[...]) * 0.125
            dv_scr[rows, :] = nn(g_turned[mine, :], p_scr[...])
        lane = lax.broadcasted_iota(jnp.int32, outs[0].shape, 1)
        dq_ref[:, cols] = (jnp.where(lane < 64, outs[0], outs[1]) * 0.125).astype(LOW)
    dk_ref[...] = dk_scr[...].T.astype(LOW)
    dv_ref[...] = dv_scr[...].T.astype(LOW)
    turned = tok[...].T
    sums[0, :, :HALF] = nn(turned, dq_ref[...])
    sums[0, :, HALF:] = nn(turned, dk_ref[...])
    sums[1, :, :HALF] = nn(turned, dv_ref[...])
    sums[1, :HALF, HALF:] = gwo[:, :HALF]
    sums[1, HALF:, HALF:] = gwo[:, HALF:]
    extra[0] = vec2[...]
    extra[0, 3:5, :] = vec3[0:2, :]
    extra[1] = vec1[...]
    extra[1, 3:4, :HALF] = jnp.sum(dq_ref[...].astype(F32), axis=0, keepdims=True)
    extra[1, 3:4, HALF:] = jnp.sum(dv_ref[...].astype(F32), axis=0, keepdims=True)
    put_turned(sums, keep, send, place[0], place[1], place[2], PIECE + 8, extra)


def entry_part_kernel(dq, dk, dv, wq, wk, wv, out):
    out[...] = nt(dq[...], wq[...])
    out[...] += nt(dk[...], wk[...])
    out[...] += nt(dv[...], wv[...])


CROSS = [(0, 3), (3, 0), (1, 2), (2, 1)]


def send_to(value, axis, shift):
    count = 2 if axis in ("w", "c", "t") else 4
    return lax.ppermute(value, axis, [(i, (i + shift) % count) for i in range(count)])


def strip_kernel(a, b, c, d, out):
    rows = a.shape[0]
    for j, part in enumerate((a, b, c, d)):
        out[j * rows : (j + 1) * rows, :] = part[...]


def near_kernel(keep, other, from_left, from_right, right, left, own):
    size = own.shape[0]
    half = size // 2
    own[...] = keep[:size, :] + other[:size, :]
    right[:half, :] = keep[size : size + half, :] + other[size : size + half, :] + from_left[...]
    right[half:, :] = keep[size + half : 2 * size, :] + other[size + half : 2 * size, :]
    left[:half, :] = keep[3 * size : 3 * size + half, :] + other[3 * size : 3 * size + half, :]
    left[half:, :] = keep[3 * size + half :, :] + other[3 * size + half :, :] + from_right[...]


def split_kernel(own, one, two, *outs):
    rows = outs[0].shape[0]
    for j, out in enumerate(outs):
        at = slice(j * rows, (j + 1) * rows)
        out[...] = own[at, :] + one[at, :] + two[at, :]


class Group:
    def __init__(self, keep, send, big, small):
        self.keep, self.send, self.big, self.small = keep, send, big, small

    def core(self):
        self.other = send_to(self.send, "c", 1)

    def far(self):
        size = self.keep.shape[0] // 4
        half = size // 2
        top, low = slice(2 * size, 2 * size + half), slice(2 * size + half, 3 * size)
        self.from_left = send_to(self.keep[top] + self.other[top], self.big, 1)
        self.from_right = send_to(self.keep[low] + self.other[low], self.big, -1)

    def near(self):
        size = self.keep.shape[0] // 4
        right, left, self.own = run(
            near_kernel, (shaped(size, DIM),) * 3, None, (self.keep, self.other, self.from_left, self.from_right), cost=1e8
        )
        self.one, self.two = send_to(right, self.big, 1), send_to(left, self.big, -1)

    def direct(self):
        rows = self.own.shape[0] // 4
        strips = run(split_kernel, (shaped(rows, DIM),) * 4, None, (self.own, self.one, self.two), cost=1e8)
        self.strips = (
            strips[0],
            send_to(strips[1], self.small, 1),
            send_to(strips[2], self.small, 2),
            send_to(strips[3], self.small, -1),
        )

    def pair(self):
        one, two, three, four = self.strips
        self.piece = (one + two) + (three + four)
        self.twin = send_to(self.piece, "w", 1)

    def gather_small(self):
        self.fan_out(self.piece + self.twin)

    def fan_out(self, piece):
        self.parts = (
            piece,
            send_to(piece, self.small, -1),
            send_to(piece, self.small, 2),
            send_to(piece, self.small, 1),
        )

    def gather_near(self):
        self.strip = run(strip_kernel, shaped(4 * self.parts[0].shape[0], DIM), None, self.parts, cost=1e8)
        self.right, self.left = send_to(self.strip, self.big, -1), send_to(self.strip, self.big, 1)
        self.their_strip = send_to(self.strip, "c", 1)

    def gather_far(self):
        half = self.strip.shape[0] // 2
        self.far_top = send_to(self.left[:half], self.big, 1)
        self.far_low = send_to(self.right[half:], self.big, -1)
        self.their_near = send_to(self.right, "c", 1), send_to(self.left, "c", 1)

    def gather_core(self):
        self.their_far = send_to(self.far_top, "c", 1), send_to(self.far_low, "c", 1)

    def pieces(self):
        mine = (self.strip, self.right, self.left, self.far_top, self.far_low)
        return mine + (self.their_strip,) + self.their_near + self.their_far

    def finish(self, kernel, outs, place):
        self.gather_core()
        return run(kernel, outs, place, self.pieces(), cost=1e8, spare=12)


def tie(*groups):
    flat, tree = jax.tree.flatten(groups)
    return jax.tree.unflatten(tree, lax.optimization_barrier(flat))


def each_piece(pieces, big, small, rows):
    own, right, left, far_top, far_low = pieces
    for turn, source, start, count in ((0, own, 0, 4), (1, right, 0, 4), (3, left, 0, 4), (2, far_top, 0, 2), (2, far_low, 2, 2)):
        for j in range(count):
            at_big, at_small = (big + turn) & 3, (small + start + j) & 3
            yield source, j * rows, at_big, at_small


def row_of(at_big, at_small):
    return pl.ds(pl.multiple_of(at_big * (4 * PIECE) + at_small * PIECE, PIECE), PIECE)


def down_out_kernel(place, *refs):
    pieces, out = refs[:10], refs[10]
    core, big, small = place[0], place[1], place[2]
    for side, half in ((pieces[:5], core), (pieces[5:], 1 - core)):
        for source, first, at_big, at_small in each_piece(side, big, small, PIECE):
            out[half, row_of(at_big, at_small), :] = source[first : first + PIECE, :]


def up_out_kernel(place, *refs):
    pieces, out = refs[:10], refs[10]
    core, big, small = place[0], place[1], place[2]
    for side, half in ((pieces[:5], core), (pieces[5:], 1 - core)):
        columns = pl.ds(pl.multiple_of(half * DIM, DIM), DIM)
        for source, first, at_big, at_small in each_piece(side, big, small, PIECE):
            out[row_of(at_big, at_small), columns] = source[first : first + PIECE, :]


def side_out_kernel(place, *refs):
    pieces, (qw, kw, vw, ow, vec) = refs[:10], refs[10:]
    core, big, small = place[0], place[1], place[2]
    rows = PIECE + 8

    def copy_all(first_half, second_half):
        for half, side in ((0, first_half), (1, second_half)):
            for source, first, at_big, at_small in each_piece(side, big, small, rows):
                body = slice(first, first + PIECE)
                at = row_of(at_big, at_small)
                if half == 0:
                    qw[at, :] = source[body, :HALF]
                    kw[at, :] = source[body, HALF:]
                else:
                    vw[at, :] = source[body, :HALF]
                    row = pl.ds(pl.multiple_of((at_big & 1) * (4 * PIECE) + at_small * PIECE, PIECE), PIECE)
                    ow[row, pl.ds(pl.multiple_of((at_big >> 1) * HALF, HALF), HALF)] = source[body, HALF:]

                @pl.when((at_big + at_small) == 0)
                def _(source=source, first=first, half=half):
                    vec[half] = source[first + PIECE : first + rows, :]

    @pl.when(core == 0)
    def _():
        copy_all(pieces[:5], pieces[5:])

    @pl.when(core == 1)
    def _():
        copy_all(pieces[5:], pieces[:5])


def on_device(
    tokens,
    seg_ids,
    pad_mask,
    query_weight,
    query_bias,
    key_weight,
    value_weight,
    value_bias,
    out_weight,
    out_bias,
    first_gain,
    first_shift,
    up_weight,
    up_bias,
    down_weight,
    down_bias,
    second_gain,
    second_shift,
    cotangent,
):
    tok = tokens.reshape(LEN, DIM)
    cot = cotangent.reshape(LEN, DIM)
    at_x, at_z, at_c = (lax.axis_index(name) for name in ("x", "z", "c"))
    place_xz = jnp.stack([at_c, at_x, at_z]).astype(jnp.int32)
    place_zx = jnp.stack([at_c, at_z, at_x]).astype(jnp.int32)
    row = lambda vector: vector.reshape(1, -1)
    ob, g1, s1, db, g2, s2 = (row(v) for v in (out_bias, first_gain, first_shift, down_bias, second_gain, second_shift))
    segs = (seg_ids.reshape(LEN, 1), seg_ids.reshape(1, LEN), pad_mask.reshape(1, LEN))
    ub = up_bias.reshape(2, DIM)
    mat = lambda *shape: pltpu.VMEM(shape, F32)
    low_mat = lambda *shape: pltpu.VMEM(shape, LOW)

    up_shard = lax.dynamic_slice(up_weight, ((at_z * 4 + at_x) * PIECE, at_c * DIM), (PIECE, DIM)).astype(F32)
    down_shard = lax.dynamic_slice(down_weight, (at_c * DIM + (at_x * 4 + at_z) * PIECE, 0), (PIECE, DIM)).astype(F32)
    up_fetch, down_fetch = Group(None, None, "z", "x"), Group(None, None, "x", "z")
    up_shard = lax.ppermute(up_shard, ("w", "t"), CROSS)
    down_shard = lax.ppermute(down_shard, ("w", "t"), CROSS)
    q, k, v, att, lse, part = run(
        attend_kernel,
        (shaped(LEN, HALF, kind=LOW),) * 4 + (shaped(LEN, 128), shaped(LEN + 8, DIM)),
        None,
        segs + (tok, query_weight, key_weight, value_weight, row(query_bias), row(value_bias), out_weight, jnp.pad(ub, ((0, 6), (0, 0)))),
        [mat(LEN, LEN), mat(LEN, LEN), low_mat(LEN, LEN)],
        cost=6e9,
    )
    part, up_shard, down_shard = tie(part, up_shard, down_shard)
    part_other = send_to(part, "t", 1)
    up_fetch.fan_out(up_shard)
    down_shard, up_fetch.parts = tie(down_shard, up_fetch.parts)
    up_fetch.gather_near()
    down_fetch.fan_out(down_shard)
    down_fetch.parts, up_fetch.strip = tie(down_fetch.parts, up_fetch.strip)
    down_fetch.gather_near()
    up_fetch.right, up_fetch.left = tie(up_fetch.right, up_fetch.left)
    up_fetch.gather_far()
    up_fetch.far_top, up_fetch.far_low, down_fetch.right, down_fetch.left = tie(
        up_fetch.far_top, up_fetch.far_low, down_fetch.right, down_fetch.left
    )
    up_fetch.gather_core()
    down_fetch.gather_far()
    part, part_other, up_pieces = tie(part, part_other, up_fetch.pieces())
    low, zhat1, r1, act_own, act_oth, dg_own, dg_oth, wup_oth = run(
        up_kernel,
        (
            shaped(LEN, DIM, kind=LOW),
            shaped(LEN, DIM),
            shaped(LEN, 1),
            shaped(LEN, 2 * DIM, kind=LOW),
            shaped(LEN, 2 * DIM, kind=LOW),
            shaped(LEN, 2 * DIM),
            shaped(LEN, 2 * DIM),
            shaped(2, DIM, DIM, kind=LOW),
        ),
        place_zx,
        (part, part_other, tok, ob, g1, s1, up_weight, ub) + up_pieces,
        [mat(LEN, 256)],
        cost=1e10,
    )
    down_fetch.gather_core()
    mixed, sgrad, slow, vec2, wdown_oth = run(
        down_kernel,
        (shaped(LEN, DIM, kind=LOW), shaped(LEN, DIM), shaped(LEN, DIM, kind=LOW), shaped(8, DIM), shaped(2, DIM, DIM, kind=LOW)),
        place_xz,
        (zhat1, g1, s1, act_own, act_oth, down_weight, db, g2, s2, cot) + down_fetch.pieces(),
        [mat(LEN, DIM), mat(LEN, DIM), mat(3, 8, DIM)],
        cost=6e9,
    )
    turned = (shaped(16 * PIECE, DIM),) * 2
    down = Group(*run(down_grad_kernel, turned, place_xz, (act_own, slow), [mat(2, DIM, DIM)], cost=3e9), "x", "z")
    down.core()
    down.keep, slow = tie(down.keep, slow)
    ug_own, vec3, up_keep, up_send = run(
        up_grad_kernel,
        (shaped(LEN, 2 * DIM, kind=LOW), shaped(8, DIM)) + turned,
        place_zx,
        (slow, down_weight, dg_own, low),
        [mat(2, DIM, DIM), mat(LEN, DIM), mat(2, 8, DIM)],
        cost=5e9,
    )
    down.other, ug_own = tie(down.other, ug_own)
    down.far()
    up = Group(up_keep, up_send, "z", "x")
    up.core()
    first_grad, attg, gwo, vec1 = run(
        entry_kernel,
        (shaped(LEN, DIM), shaped(LEN, HALF, kind=LOW), shaped(HALF, DIM), shaped(8, DIM)),
        None,
        (slow, wdown_oth, dg_oth, up_weight, wup_oth, ug_own, sgrad, zhat1, r1, g1, att, out_weight),
        [mat(LEN, DIM), low_mat(LEN, DIM), mat(LEN, DIM), mat(LEN, DIM), low_mat(LEN, DIM), mat(3, 8, DIM)],
        cost=8e9,
    )
    attg, down.from_left, down.from_right, up.other = tie(attg, down.from_left, down.from_right, up.other)
    down.near()
    up.far()
    dq, dk, dv, side_keep, side_send = run(
        attend_back_kernel,
        (shaped(LEN, HALF, kind=LOW),) * 3 + (shaped(16 * (PIECE + 8), DIM),) * 2,
        place_xz,
        segs + (q, k, v, attg, lse, tok, gwo, vec1, vec2, vec3),
        [
            mat(LEN, LEN),
            mat(LEN, LEN),
            mat(LEN, LEN),
            low_mat(LEN, LEN),
            low_mat(LEN, LEN),
            mat(HALF, LEN),
            mat(HALF, LEN),
            mat(2, DIM, DIM),
            mat(2, 8, DIM),
        ],
        cost=1e10,
    )
    side = Group(side_keep, side_send, "x", "z")
    side.send, dq, down.one, down.two, up.from_left, up.from_right = tie(
        side.send, dq, down.one, down.two, up.from_left, up.from_right
    )
    side.core()
    down.direct()
    up.near()
    entry = run(entry_part_kernel, shaped(LEN, DIM), None, (dq, dk, dv, query_weight, key_weight, value_weight), cost=2e9)
    side.other, down.strips, entry = tie(side.other, down.strips, entry)
    side.far()
    down.pair()
    side.from_left, side.from_right, down.twin, up.one, up.two = tie(side.from_left, side.from_right, down.twin, up.one, up.two)
    side.near()
    down.gather_small()
    up.direct()
    down.parts, up.strips = tie(down.parts, up.strips)
    up.pair()
    down.gather_near()
    up.twin, side.one, side.two = tie(up.twin, side.one, side.two)
    side.direct()
    up.gather_small()
    down.right, down.left, up.parts, side.strips = tie(down.right, down.left, up.parts, side.strips)
    side.pair()
    down.gather_far()
    up.gather_near()
    side.twin, entry, down.far_top, down.far_low = tie(side.twin, entry, down.far_top, down.far_low)
    side.gather_small()
    entry_other = send_to(entry, "t", 1)
    side.parts, up.right, up.left = tie(side.parts, up.right, up.left)
    side.gather_near()
    up.gather_far()
    down_sum = down.finish(down_out_kernel, shaped(2, DIM, DIM), place_xz)
    side.right, side.left, up.far_top, up.far_low = tie(side.right, side.left, up.far_top, up.far_low)
    side.gather_far()
    up_sum = up.finish(up_out_kernel, shaped(DIM, 2 * DIM), place_zx)
    side.far_top, side.far_low, up_sum = tie(side.far_top, side.far_low, up_sum)
    weight = shaped(DIM, HALF)
    qw, kw, vw, ow, vec = side.finish(
        side_out_kernel, (weight, weight, weight, shaped(HALF, DIM), shaped(2, 8, DIM)), place_xz
    )
    input_gradient = first_grad + (entry + entry_other)
    return (
        mixed.reshape(1, LEN, DIM),
        input_gradient.reshape(1, LEN, DIM),
        qw,
        vec[1, 3, :HALF],
        kw,
        vw,
        vec[1, 3, HALF:],
        ow,
        vec[1, 0],
        vec[1, 1],
        vec[1, 2],
        up_sum,
        vec[0, 3:5].reshape(2 * DIM),
        down_sum.reshape(2 * DIM, DIM),
        vec[0, 0],
        vec[0, 1],
        vec[0, 2],
    )


ROWS_AXES = ("x", "w", "z", "c")


def solution(mesh):
    fine = jax.sharding.Mesh(mesh.devices.reshape(4, 2, 4, 2, 2), ROWS_AXES + ("t",))
    by_row, ids = P(ROWS_AXES, None, None), P(ROWS_AXES, None)
    columns, units, rows, whole = P(None, "t"), P("t"), P("t", None), P()
    return jax.shard_map(
        on_device,
        mesh=fine,
        in_specs=(
            (by_row, ids, ids, columns, units, columns, columns, units, rows)
            + (whole, whole, whole, columns, units, rows, whole, whole, whole, by_row)
        ),
        out_specs=(
            (by_row, by_row, columns, units, columns, columns, units, rows)
            + (whole, whole, whole, columns, units, rows, whole, whole, whole)
        ),
        check_vma=False,
    )
```

```python
import math

import jax
import jax.numpy as jnp
from jax import lax
from jax.experimental import pallas as pl
from jax.experimental.pallas import tpu as pltpu
from jax.sharding import PartitionSpec as P

EPSILON = 1e-06
NEG_LARGE = -1e30
LOW = jnp.bfloat16
F32 = jnp.float32
LEN = 512
DIM = 768
HALF = 384
HEADS = 6
STEP = 32
PIECE = 48
LANES = 128
EARLY_ROWS = 6 * PIECE + 6 * (PIECE // 2)
LATE_ROWS = 6 * (PIECE // 2) + 3 * (PIECE // 2) + 9 * (PIECE // 2) + 8
VMEM = pl.BlockSpec(memory_space=pltpu.VMEM)
SMEM = pl.BlockSpec(memory_space=pltpu.SMEM)
ANY = pl.BlockSpec(memory_space=pl.ANY)
FAR = pl.BlockSpec(memory_space=pltpu.HBM)


def nn(left_op, right_op):
    return jnp.dot(left_op, right_op, preferred_element_type=F32)


def nt(left_op, right_op):
    return lax.dot_general(left_op, right_op, (((1,), (1,)), ((), ())), preferred_element_type=F32)


def tn(left_op, right_op):
    return lax.dot_general(left_op, right_op, (((0,), (0,)), ((), ())), preferred_element_type=F32)


def shaped(*shape, kind=F32):
    return jax.ShapeDtypeStruct(shape, kind)


def run(kernel, outs, place, args, scratch=(), spare=8, far=0, after=()):
    after = tuple(jax.tree.leaves(after))
    args = tuple(pltpu.with_memory_space_constraint(arg, pltpu.HBM) for arg in args[:far]) + tuple(args[far:])
    head = () if place is None else (place,)
    in_specs = [SMEM] * len(head) + [FAR] * far + [VMEM] * (len(args) - far) + [ANY] * len(after)
    reads, writes = len(head) + len(args), len(head) + len(args) + len(after)

    def body(*refs):
        kernel(*refs[:reads], *refs[writes:])

    need = sum(math.prod(s.shape) * jnp.dtype(s.dtype).itemsize for s in scratch if s.dtype in (F32, LOW))
    return pl.pallas_call(
        body,
        out_shape=outs,
        in_specs=in_specs,
        out_specs=jax.tree.map(lambda _: VMEM, outs),
        scratch_shapes=scratch,
        name=kernel.__name__,
        compiler_params=pltpu.CompilerParams(vmem_limit_bytes=need + (spare << 20)),
        cost_estimate=pl.CostEstimate(flops=1, bytes_accessed=1, transcendentals=0),
    )(*head, *args, *after)


def over_rows(body, count=LEN // STEP, unroll=LEN // STEP):
    def step(i, carry):
        body(pl.ds(pl.multiple_of(i * STEP, STEP), STEP), i)
        return carry

    lax.fori_loop(0, count, step, 0, unroll=unroll)


def fold(values):
    return jnp.sum(values.reshape(STEP // 8, 8, values.shape[-1]), axis=0)


def fill_bias(seg_row, pad_row, bias):
    spread = jnp.broadcast_to(seg_row[...].astype(F32), (LANES, LEN)).T[:, 0:1]
    for i in range(LEN // STEP):
        down = lax.broadcasted_iota(jnp.int32, (STEP, LEN), 0) + i * STEP
        across = lax.broadcasted_iota(jnp.int32, (STEP, LEN), 1)
        same = (spread[i * STEP : (i + 1) * STEP] == seg_row[...].astype(F32)) & (pad_row[...] == 1)
        bias[i * STEP : (i + 1) * STEP, :] = jnp.where(same | (down == across), 0.0, NEG_LARGE)


def head_of(pair, head):
    lane = lax.broadcasted_iota(jnp.int32, pair.shape, 1)
    return jnp.where((lane < 64) == (head == 0), pair.astype(F32), 0.0)


def attend_kernel(
    tok_far, wq_far, wk_far, wv_far, wo_far, seg_row, pad_row, qb, vb, ub,
    q_ref, k_ref, v_ref, att_ref, lse_ref, part_ref, bias, s_scr, p_scr, tok, wq, wk, wv, wo, sems,
):
    pairs = ((tok_far, tok), (wq_far, wq), (wk_far, wk), (wv_far, wv), (wo_far, wo))
    copies = [pltpu.make_async_copy(far, near, sems.at[j]) for j, (far, near) in enumerate(pairs)]
    for copy in copies:
        copy.start()
    fill_bias(seg_row, pad_row, bias)
    copies[0].wait()
    tokens = tok[...]
    copies[1].wait()
    q_ref[...] = (nn(tokens, wq[...]) + qb[...].reshape(1, HALF)).astype(LOW)
    copies[2].wait()
    k_ref[...] = nn(tokens, wk[...]).astype(LOW)
    copies[3].wait()
    v_ref[...] = (nn(tokens, wv[...]) + vb[...].reshape(1, HALF)).astype(LOW)
    for pair in range(HEADS // 2):
        cols = slice(pair * 128, pair * 128 + 128)
        outs = []
        for head in range(2):
            s_scr[...] = nt((head_of(q_ref[:, cols], head) * 0.125).astype(LOW), k_ref[:, cols])
            column = 2 * pair + head

            def body(rows, i, column=column):
                scores = s_scr[rows, :] + bias[rows, :]
                peak = jnp.max(scores, axis=-1, keepdims=True)
                grown = jnp.exp(scores - peak)
                total = jnp.sum(grown, axis=-1, keepdims=True)
                p_scr[rows, :] = (grown * (1.0 / total)).astype(LOW)
                lse_ref[rows, column : column + 1] = peak + jnp.log(total)

            over_rows(body)
            outs.append(nn(p_scr[...], v_ref[:, cols]))
        lane = lax.broadcasted_iota(jnp.int32, outs[0].shape, 1)
        att_ref[:, cols] = jnp.where(lane < 64, outs[0], outs[1]).astype(LOW)
    copies[4].wait()
    part_ref[:LEN, :] = nn(att_ref[...], wo[...])
    part_ref[LEN:, :] = jnp.zeros((8, DIM), F32)
    for half in range(2):
        part_ref[LEN + half : LEN + half + 1, :] = ub[half * DIM : (half + 1) * DIM].reshape(1, DIM)


def place_pieces(dst, pieces, big, small, offset):
    for source, first, at_big, at_small in each_piece(pieces, big, small, 2 * PIECE):
        dst[rows_at(at_big, at_small, PIECE), :] = source[first + offset : first + offset + PIECE, :].astype(LOW)


def up_kernel(
    place, mine, theirs, tok, ob, g1, s1, wup, *rest
):
    pieces, rest = rest[:10], rest[10:]
    low_ref, zhat_ref, r_ref, act_own, act_oth, dg_own, dg_oth, wup_oth, u_scr = rest
    core, big, small = place[0], place[1], place[2]
    place_pieces(wup_oth.at[core], pieces[:5], big, small, 0)
    place_pieces(wup_oth.at[1 - core], pieces[5:], small, big, 0)

    def norm(rows, i):
        z = tok[rows, :].astype(F32) + (mine[rows, :] + theirs[rows, :]) + ob[...]
        center = z - jnp.mean(z, axis=-1, keepdims=True)
        r = lax.rsqrt(jnp.mean(center * center, axis=-1, keepdims=True) + EPSILON)
        zhat = center * r
        zhat_ref[rows, :] = zhat
        r_ref[rows, :] = r
        low_ref[rows, :] = (zhat * g1[...] + s1[...]).astype(LOW)

    over_rows(norm)
    for side in range(2):
        for half in range(2):
            for chunk in range(3):
                cols = slice(chunk * 256, chunk * 256 + 256)
                wide = slice(half * DIM + chunk * 256, half * DIM + chunk * 256 + 256)
                if side == 0:
                    weight, bias, act, dg = wup[:, wide], mine[LEN + half : LEN + half + 1, cols], act_own, dg_own
                else:
                    weight, bias, act, dg = wup_oth[half, :, cols], theirs[LEN + half : LEN + half + 1, cols], act_oth, dg_oth
                u_scr[...] = nn(low_ref[...], weight) + bias

                def gelu(rows, i, act=act, dg=dg, wide=wide):
                    u = u_scr[rows, :]
                    cdf = 0.5 + 0.5 * lax.erf(u * (0.5**0.5))
                    act[rows, wide] = (u * cdf).astype(LOW)
                    dg[rows, wide] = cdf + u * (jnp.exp(-0.5 * (u * u)) * 0.3989422804014327)

                over_rows(gelu)


def down_kernel(
    place, zhat1, g1, s1, act_own, act_oth, wdown, db, g2, s2, cot, *rest
):
    pieces, rest = rest[:10], rest[10:]
    mixed_ref, sgrad_ref, slow_ref, vec_ref, wdown_oth, own_scr, oth_scr, acc = rest
    core, big, small = place[0], place[1], place[2]
    place_pieces(wdown_oth.at[core], pieces[:5], big, small, PIECE)
    place_pieces(wdown_oth.at[1 - core], pieces[5:], small, big, PIECE)
    own_scr[...] = nn(act_own[:, :DIM], wdown[:DIM, :])
    own_scr[...] += nn(act_own[:, DIM:], wdown[DIM:, :])
    oth_scr[...] = nn(act_oth[:, :DIM], wdown_oth[0])
    oth_scr[...] += nn(act_oth[:, DIM:], wdown_oth[1])
    acc[...] = jnp.zeros_like(acc)

    def body(rows, i):
        hidden = zhat1[rows, :] * g1[...] + s1[...]
        z = hidden + (own_scr[rows, :] + oth_scr[rows, :]) + db[...]
        center = z - jnp.mean(z, axis=-1, keepdims=True)
        r = lax.rsqrt(jnp.mean(center * center, axis=-1, keepdims=True) + EPSILON)
        zhat = center * r
        mixed_ref[rows, :] = (zhat * g2[...] + s2[...]).astype(LOW)
        g = cot[rows, :].astype(F32)
        u = g * g2[...]
        grad = r * (u - jnp.mean(u, axis=-1, keepdims=True) - zhat * jnp.mean(u * zhat, axis=-1, keepdims=True))
        sgrad_ref[rows, :] = grad
        slow_ref[rows, :] = grad.astype(LOW)
        acc[0] += fold(grad)
        acc[1] += fold(g * zhat)
        acc[2] += fold(g)

    over_rows(body)
    put_sums(vec_ref, acc, 3)


def put_sums(vec_ref, acc, count):
    vec_ref[...] = jnp.zeros_like(vec_ref)
    for k in range(count):
        vec_ref[k : k + 1, :] = jnp.sum(acc[k], axis=0, keepdims=True)


def each_place(place, keep, send):
    core, big, small = place[0], place[1], place[2]
    for target, half, first, second in ((keep, core, big, small), (send, 1 - core, small, big)):
        for j in range(4):
            for k in range(4):
                yield target, half, 4 * j + k, (first + j) & 3, (second + k) & 3


def rows_at(at_big, at_small, rows):
    return pl.ds(pl.multiple_of(at_big * (4 * rows) + at_small * rows, rows), rows)


def pack(target, start, values):
    rows = values.shape[0]
    for block in range(values.shape[1] // LANES):
        target[start + block * rows : start + (block + 1) * rows, :] = values[:, block * LANES : (block + 1) * LANES]


def early_grad_kernel(place, act_own, slow, low, ug_own, keep, send, downs, ups):
    for half in range(2):
        wide = slice(half * DIM, half * DIM + DIM)
        downs[half] = tn(act_own[:, wide], slow[...])
        ups[half] = tn(low[:, :HALF], ug_own[:, wide])
    for target, half, number, at_big, at_small in each_place(place, keep, send):
        start = number * EARLY_ROWS
        pack(target, start, downs[half, rows_at(at_big, at_small, PIECE), :])
        pack(target, start + 6 * PIECE, ups[half, rows_at(at_big, at_small, PIECE // 2), :])


def unit_kernel(slow, wdown, dg_own, ug_ref, vec_ref, a_scr, acc):
    acc[...] = jnp.zeros_like(acc)
    vec_ref[...] = jnp.zeros_like(vec_ref)
    for half in range(2):
        wide = slice(half * DIM, half * DIM + DIM)
        a_scr[...] = nt(slow[...], wdown[wide, :])

        def body(rows, i, half=half, wide=wide):
            grad = (a_scr[rows, :] * dg_own[rows, wide]).astype(LOW)
            ug_ref[rows, wide] = grad
            acc[half] += fold(grad.astype(F32))

        over_rows(body)
        vec_ref[half : half + 1, :] = jnp.sum(acc[half], axis=0, keepdims=True)


def entry_kernel(
    slow, wdown_oth, dg_oth, wup, wup_oth, ug_own, sgrad, zhat1, r1, g1, att, wo, vec2, vec3,
    first_ref, attg_ref, gwo_ref, vec_ref, a_scr, ug_scr, own_scr, oth_scr, low_scr, acc,
):
    acc[...] = jnp.zeros_like(acc)
    own_scr[...] = nt(ug_own[:, :DIM], wup[:, :DIM])
    own_scr[...] += nt(ug_own[:, DIM:], wup[:, DIM:])
    for half in range(2):
        wide = slice(half * DIM, half * DIM + DIM)
        a_scr[...] = nt(slow[...], wdown_oth[half])

        def body(rows, i, wide=wide):
            ug_scr[rows, :] = (a_scr[rows, :] * dg_oth[rows, wide]).astype(LOW)

        over_rows(body)
        if half == 0:
            oth_scr[...] = nt(ug_scr[...], wup_oth[half])
        else:
            oth_scr[...] += nt(ug_scr[...], wup_oth[half])

    def norm(rows, i):
        g = sgrad[rows, :] + (own_scr[rows, :] + oth_scr[rows, :])
        zhat = zhat1[rows, :]
        u = g * g1[...]
        grad = r1[rows, :] * (u - jnp.mean(u, axis=-1, keepdims=True) - zhat * jnp.mean(u * zhat, axis=-1, keepdims=True))
        first_ref[rows, :] = grad
        low_scr[rows, :] = grad.astype(LOW)
        acc[0] += fold(grad)
        acc[1] += fold(g * zhat)
        acc[2] += fold(g)

    over_rows(norm)
    vec_ref[0:3, :] = vec2[0:3, :]
    for k in range(3):
        vec_ref[3 + k : 4 + k, :] = jnp.sum(acc[k], axis=0, keepdims=True)
    vec_ref[6:8, :] = vec3[0:2, :]
    attg_ref[...] = nt(low_scr[...], wo[...]).astype(LOW)
    gwo_ref[...] = tn(att[...], low_scr[...])


def attend_back(bias, q, k, v, attg, lse, pair, s_scr, g_scr, p_scr, d_scr, dk_scr, dv_scr):
    cols = slice(pair * 128, pair * 128 + 128)
    q_turned = q[:, cols].T
    g_turned = attg[:, cols].T
    outs = []
    for head in range(2):
        s_scr[...] = nt((head_of(q[:, cols], head) * 0.125).astype(LOW), k[:, cols])
        g_scr[...] = nt(head_of(attg[:, cols], head).astype(LOW), v[:, cols])
        column = 2 * pair + head

        def body(rows, i, column=column):
            attention = jnp.exp(s_scr[rows, :] + bias[rows, :] - lse[rows, column : column + 1])
            grad = g_scr[rows, :]
            p_scr[rows, :] = attention.astype(LOW)
            inner = jnp.sum(grad * attention, axis=-1, keepdims=True)
            d_scr[rows, :] = (attention * (grad - inner)).astype(LOW)

        over_rows(body)
        mine = slice(64 * head, 64 * head + 64)
        outs.append(nn(d_scr[...], k[:, cols]))
        dk_scr[mine, :] = nn(q_turned[mine, :], d_scr[...]) * 0.125
        dv_scr[mine, :] = nn(g_turned[mine, :], p_scr[...])
    lane = lax.broadcasted_iota(jnp.int32, outs[0].shape, 1)
    dq = (jnp.where(lane < 64, outs[0], outs[1]) * 0.125).astype(LOW)
    return dq, dk_scr[...].T.astype(LOW), dv_scr[...].T.astype(LOW)


def attend_back_kernel(bias, q, k, v, attg, lse, dq_ref, dk_ref, dv_ref, *scr):
    for pair in range(HEADS // 2):
        cols = slice(pair * 128, pair * 128 + 128)
        dq_ref[:, cols], dk_ref[:, cols], dv_ref[:, cols] = attend_back(bias, q, k, v, attg, lse, pair, *scr)


def late_grad_kernel(place, tok, dq, dk, dv, low, ug_own, gwo, vec, keep, send, ups, outs, sums, extra):
    for half in range(2):
        ups[half] = tn(low[:, HALF:], ug_own[:, half * DIM : (half + 1) * DIM])
        outs[half] = gwo[:, half * HALF : (half + 1) * HALF]
    extra[...] = jnp.zeros_like(extra)
    for block in range(DIM // LANES):
        extra[0, block] = vec[:, block * LANES : (block + 1) * LANES]
    turned = tok[...].T
    for number, grads in enumerate((dq, dk, dv)):
        at = slice(number * HALF, number * HALF + HALF)
        total = nn(turned, grads[...])
        sums[0, :, at] = total[:HALF]
        sums[1, :, at] = total[HALF:]
        if number != 1:
            bias_grad = jnp.sum(grads[...].astype(F32), axis=0, keepdims=True)
            for block in range(3):
                row = number // 2 * 3 + block
                extra[0, 6, row : row + 1, :] = bias_grad[:, block * LANES : (block + 1) * LANES]
    for target, half, number, at_big, at_small in each_place(place, keep, send):
        at = rows_at(at_big, at_small, PIECE // 2)
        start = number * LATE_ROWS
        pack(target, start, ups[half, at, :])
        pack(target, start + 3 * PIECE, outs[half, at, :])
        pack(target, start + 9 * (PIECE // 2), sums[half, at, :])
        target[start + LATE_ROWS - 8 : start + LATE_ROWS, :] = extra[half, at_big * 4 + at_small]


def entry_part_kernel(dq, dk, dv, wq, wk, wv, out):
    out[...] = nt(dq[...], wq[...])
    out[...] += nt(dk[...], wk[...])
    out[...] += nt(dv[...], wv[...])


CROSS = [(0, 3), (3, 0), (1, 2), (2, 1)]


def send_to(value, axis, shift):
    count = 2 if axis in ("w", "c", "t") else 4
    return lax.ppermute(value, axis, [(i, (i + shift) % count) for i in range(count)])


def send_along(value, big, shift):
    pairs = []
    for x in range(4):
        for z in range(4):
            for core in range(2):
                to_x, to_z = ((x + shift) % 4, z) if (core == 0) == big else (x, (z + shift) % 4)
                pairs.append((x * 8 + z * 2 + core, to_x * 8 + to_z * 2 + core))
    return lax.ppermute(value, ("x", "z", "c"), pairs)


def far_kernel(keep, other, right, left):
    half = right.shape[0]
    right[...] = keep[4 * half : 5 * half, :] + other[4 * half : 5 * half, :]
    left[...] = keep[5 * half : 6 * half, :] + other[5 * half : 6 * half, :]


def near_kernel(keep, other, from_left, from_right, right, left, own):
    size = own.shape[0]
    half = size // 2
    own[...] = keep[:size, :] + other[:size, :]
    right[:half, :] = keep[size : size + half, :] + other[size : size + half, :] + from_left[...]
    right[half:, :] = keep[size + half : 2 * size, :] + other[size + half : 2 * size, :]
    left[:half, :] = keep[3 * size : 3 * size + half, :] + other[3 * size : 3 * size + half, :]
    left[half:, :] = keep[3 * size + half :, :] + other[3 * size + half :, :] + from_right[...]


def split_kernel(own, one, two, *outs):
    rows = outs[0].shape[0]
    for j, out in enumerate(outs):
        at = slice(j * rows, (j + 1) * rows)
        out[...] = own[at, :] + one[at, :] + two[at, :]


def piece_kernel(one, two, three, four, out):
    out[...] = (one[...] + two[...]) + (three[...] + four[...])


def twin_kernel(one, two, out):
    out[...] = one[...] + two[...]


def strip_kernel(a, b, c, d, out):
    rows = a.shape[0]
    for j, part in enumerate((a, b, c, d)):
        out[j * rows : (j + 1) * rows, :] = part[...]


def halves_kernel(left, right, top, low):
    half = top.shape[0]
    top[...] = left[:half, :]
    low[...] = right[half:, :]


def tie(*groups):
    flat, tree = jax.tree.flatten(groups)
    return jax.tree.unflatten(tree, lax.optimization_barrier(flat))


class Group:
    def __init__(self, keep=None, send=None):
        self.keep, self.send = keep, send

    def core(self):
        self.other = send_to(self.send, "c", 1)
        return self.send

    def far(self, *after):
        half = self.keep.shape[0] // 8
        right, left = run(far_kernel, (shaped(half, LANES),) * 2, None, (self.keep, self.other), after=after)
        self.far_parts = send_along(right, True, 1), send_along(left, True, -1)
        return left

    def near(self, *after):
        size = self.keep.shape[0] // 4
        parts = (self.keep, self.other) + self.far_parts
        right, left, self.own = run(near_kernel, (shaped(size, LANES),) * 3, None, parts, after=after)
        self.near_parts = send_along(right, True, 1), send_along(left, True, -1)
        return left

    def direct(self, *after):
        rows = self.own.shape[0] // 4
        strips = run(split_kernel, (shaped(rows, LANES),) * 4, None, (self.own,) + self.near_parts, after=after)
        self.strips = (strips[0],) + tuple(send_along(strips[j], False, j if j < 3 else -1) for j in (1, 2, 3))
        return strips[3]

    def pair(self, *after):
        self.piece = run(piece_kernel, shaped(*self.strips[0].shape), None, self.strips, after=after)
        self.twin = send_to(self.piece, "w", 1)
        return self.piece

    def gather_small(self, *after):
        return self.fan_out(run(twin_kernel, shaped(*self.piece.shape), None, (self.piece, self.twin), after=after))

    def fan_out(self, piece):
        self.parts = (piece,) + tuple(send_along(piece, False, shift) for shift in (-1, 2, 1))
        return piece

    def gather_near(self, *after):
        rows, width = self.parts[0].shape
        self.strip = run(strip_kernel, shaped(4 * rows, width), None, self.parts, after=after)
        self.right, self.left = send_along(self.strip, True, -1), send_along(self.strip, True, 1)
        self.their_strip = send_to(self.strip, "c", 1)
        return self.strip

    def gather_far(self, *after):
        half, width = self.strip.shape[0] // 2, self.strip.shape[1]
        top, low = run(halves_kernel, (shaped(half, width),) * 2, None, (self.left, self.right), after=after)
        self.far_top, self.far_low = send_along(top, True, 1), send_along(low, True, -1)
        self.their_near = send_to(self.right, "c", 1), send_to(self.left, "c", 1)
        return low

    def gather_core(self):
        self.their_far = send_to(self.far_top, "c", 1), send_to(self.far_low, "c", 1)

    def pieces(self):
        mine = (self.strip, self.right, self.left, self.far_top, self.far_low)
        return mine + (self.their_strip,) + self.their_near + self.their_far


def each_piece(pieces, big, small, rows):
    own, right, left, far_top, far_low = pieces
    for turn, source, start, count in ((0, own, 0, 4), (1, right, 0, 4), (3, left, 0, 4), (2, far_top, 0, 2), (2, far_low, 2, 2)):
        for j in range(count):
            yield source, j * rows, (big + turn) & 3, (small + start + j) & 3


def unpack(target, rows, column, source, start, count, blocks):
    for block in range(blocks):
        at = column + block * LANES
        at = slice(at, at + LANES) if isinstance(at, int) else pl.ds(pl.multiple_of(at, LANES), LANES)
        target[rows, at] = source[start + block * count : start + (block + 1) * count, :]


def early_out_kernel(place, *refs):
    pieces, (down, up) = refs[:10], refs[10:]
    core, big, small = place[0], place[1], place[2]
    for side, half, along, across in ((pieces[:5], core, big, small), (pieces[5:], 1 - core, small, big)):
        for source, first, at_big, at_small in each_piece(side, along, across, EARLY_ROWS):
            unpack(down.at[half], rows_at(at_big, at_small, PIECE), 0, source, first, PIECE, 6)
            unpack(up, rows_at(at_big, at_small, PIECE // 2), half * DIM, source, first + 6 * PIECE, PIECE // 2, 6)


def late_out_kernel(place, up_early, *refs):
    pieces, (up, out_wo, qw, kw, vw, vec, biases, tiles) = refs[:10], refs[10:]
    core, big, small = place[0], place[1], place[2]
    count = PIECE // 2
    up[:HALF, :] = up_early[...]
    for side, half, along, across in ((pieces[:5], core, big, small), (pieces[5:], 1 - core, small, big)):
        for source, first, at_big, at_small in each_piece(side, along, across, LATE_ROWS):
            row = at_big * (4 * count) + at_small * count
            rows = pl.ds(pl.multiple_of(HALF + row, count), count)
            unpack(up, rows, half * DIM, source, first, count, 6)
            unpack(out_wo, rows_at(at_big, at_small, count), half * HALF, source, first + 6 * count, count, 3)
            rows = pl.ds(pl.multiple_of(half * HALF + row, count), count)
            for number, out in enumerate((qw, kw, vw)):
                unpack(out, rows, 0, source, first + (9 + 3 * number) * count, count, 3)
            tiles[half, at_big * 4 + at_small] = source[first + LATE_ROWS - 8 : first + LATE_ROWS, :]
    for block in range(DIM // LANES):
        vec[:, block * LANES : (block + 1) * LANES] = tiles[0, block]
    biases[...] = tiles[0, 6]


def on_device(
    tokens,
    seg_ids,
    pad_mask,
    query_weight,
    query_bias,
    key_weight,
    value_weight,
    value_bias,
    out_weight,
    out_bias,
    first_gain,
    first_shift,
    up_weight,
    up_bias,
    down_weight,
    down_bias,
    second_gain,
    second_shift,
    cotangent,
):
    tok = tokens.reshape(LEN, DIM)
    cot = cotangent.reshape(LEN, DIM)
    at_x, at_z, at_c = (lax.axis_index(name) for name in ("x", "z", "c"))
    at_big, at_small = jnp.where(at_c == 0, at_x, at_z), jnp.where(at_c == 0, at_z, at_x)
    place = jnp.stack([at_c, at_big, at_small]).astype(jnp.int32)
    row = lambda vector: vector.reshape(1, -1)
    ob, g1, s1, db, g2, s2 = (row(v) for v in (out_bias, first_gain, first_shift, down_bias, second_gain, second_shift))
    mat = lambda *shape: pltpu.VMEM(shape, F32)
    low_mat = lambda *shape: pltpu.VMEM(shape, LOW)

    first = (at_big * 4 + at_small) * PIECE
    up_shard = lax.dynamic_slice(up_weight, (first, at_c * DIM), (PIECE, DIM))
    down_shard = lax.dynamic_slice(down_weight, (at_c * DIM + first, 0), (PIECE, DIM))
    shard = lax.ppermute(jnp.concatenate([up_shard, down_shard]).astype(F32), ("w", "t"), CROSS)
    fetch = Group()
    q, k, v, att, lse, part, bias = run(
        attend_kernel,
        (shaped(LEN, HALF, kind=LOW),) * 4 + (shaped(LEN, 128), shaped(LEN + 8, DIM), shaped(LEN, LEN)),
        None,
        (tok, query_weight, key_weight, value_weight, out_weight, seg_ids, pad_mask, query_bias, value_bias, up_bias),
        [mat(LEN, LEN), low_mat(LEN, LEN), low_mat(LEN, DIM)]
        + [low_mat(DIM, HALF)] * 3
        + [low_mat(HALF, DIM), pltpu.SemaphoreType.DMA((5,))],
        far=5,
    )
    part_other = send_to(part, "t", 1)
    part, shard = tie(part, shard)
    fetch.fan_out(shard)
    fetch.gather_near()
    fetch.gather_far()
    fetch.gather_core()
    low, zhat1, r1, act_own, act_oth, dg_own, dg_oth, wup_oth = run(
        up_kernel,
        (
            shaped(LEN, DIM, kind=LOW),
            shaped(LEN, DIM),
            shaped(LEN, 1),
            shaped(LEN, 2 * DIM, kind=LOW),
            shaped(LEN, 2 * DIM, kind=LOW),
            shaped(LEN, 2 * DIM),
            shaped(LEN, 2 * DIM),
            shaped(2, DIM, DIM, kind=LOW),
        ),
        place,
        (part, part_other, tok, ob, g1, s1, up_weight) + fetch.pieces(),
        [mat(LEN, 256)],
    )
    mixed, sgrad, slow, vec2, wdown_oth = run(
        down_kernel,
        (shaped(LEN, DIM, kind=LOW), shaped(LEN, DIM), shaped(LEN, DIM, kind=LOW), shaped(8, DIM), shaped(2, DIM, DIM, kind=LOW)),
        place,
        (zhat1, g1, s1, act_own, act_oth, down_weight, db, g2, s2, cot) + fetch.pieces(),
        [mat(LEN, DIM), mat(LEN, DIM), mat(3, 8, DIM)],
    )
    ug_own, vec3 = run(
        unit_kernel,
        (shaped(LEN, 2 * DIM, kind=LOW), shaped(8, DIM)),
        None,
        (slow, down_weight, dg_own),
        [mat(LEN, DIM), mat(2, 8, DIM)],
    )
    keep, send = run(
        early_grad_kernel,
        (shaped(16 * EARLY_ROWS, LANES),) * 2,
        place,
        (act_own, slow, low, ug_own),
        [mat(2, DIM, DIM), mat(2, HALF, DIM)],
    )
    early = Group(keep, send)
    after = early.core()
    first_grad, attg, gwo, vec = run(
        entry_kernel,
        (shaped(LEN, DIM), shaped(LEN, HALF, kind=LOW), shaped(HALF, DIM), shaped(8, DIM)),
        None,
        (slow, wdown_oth, dg_oth, up_weight, wup_oth, ug_own, sgrad, zhat1, r1, g1, att, out_weight, vec2, vec3),
        [mat(LEN, DIM), low_mat(LEN, DIM), mat(LEN, DIM), mat(LEN, DIM), low_mat(LEN, DIM), mat(3, 8, DIM)],
        after=after,
    )
    after = early.far(vec)
    dq, dk, dv = run(
        attend_back_kernel,
        (shaped(LEN, HALF, kind=LOW),) * 3,
        None,
        (bias, q, k, v, attg, lse),
        [mat(LEN, LEN), mat(LEN, LEN), low_mat(LEN, LEN), low_mat(LEN, LEN), mat(128, LEN), mat(128, LEN)],
        after=after,
    )
    after = early.near(dq)
    keep, send = run(
        late_grad_kernel,
        (shaped(16 * LATE_ROWS, LANES),) * 2,
        place,
        (tok, dq, dk, dv, low, ug_own, gwo, vec),
        [mat(2, HALF, DIM), mat(2, HALF, HALF), mat(2, HALF, 3 * HALF), mat(2, 16, 8, LANES)],
        after=after,
    )
    late = Group(keep, send)
    after = late.core()
    after = early.direct(after)
    after = late.far(after)
    after = early.pair(after)
    after = late.near(after)
    after = early.gather_small(after)
    after = late.direct(after)
    after = early.gather_near(after)
    after = late.pair(after)
    after = late.gather_small(after)
    entry = run(entry_part_kernel, shaped(LEN, DIM), None, (dq, dk, dv, query_weight, key_weight, value_weight), after=after)
    entry_other = send_to(entry, "t", 1)
    after = early.gather_far(entry)
    after = late.gather_near(after)
    early.gather_core()
    down_sum, up_early = run(
        early_out_kernel, (shaped(2, DIM, DIM), shaped(HALF, 2 * DIM)), place, early.pieces(), spare=14, after=after
    )
    input_gradient = first_grad + (entry + entry_other)
    late.gather_far(up_early)
    late.gather_core()
    weight = shaped(DIM, HALF)
    up_sum, ow, qw, kw, vw, vec, biases = run(
        late_out_kernel,
        (shaped(DIM, 2 * DIM), shaped(HALF, DIM), weight, weight, weight, shaped(8, DIM), shaped(8, LANES)),
        place,
        (up_early,) + late.pieces(),
        [mat(2, 16, 8, LANES)],
        spare=18,
    )
    db, sg, ss, ob, fg, fs = (vec[j] for j in range(6))
    return (
        mixed.reshape(1, LEN, DIM),
        input_gradient.reshape(1, LEN, DIM),
        qw,
        biases[0:3].reshape(HALF),
        kw,
        vw,
        biases[3:6].reshape(HALF),
        ow,
        ob,
        fg,
        fs,
        up_sum,
        vec[6:8].reshape(2 * DIM),
        down_sum.reshape(2 * DIM, DIM),
        db,
        sg,
        ss,
    )


ROWS_AXES = ("x", "w", "z", "c")


def solution(mesh):
    fine = jax.sharding.Mesh(mesh.devices.reshape(4, 2, 4, 2, 2), ROWS_AXES + ("t",))
    by_row, ids = P(ROWS_AXES, None, None), P(ROWS_AXES, None)
    columns, units, rows, whole = P(None, "t"), P("t"), P("t", None), P()
    return jax.shard_map(
        on_device,
        mesh=fine,
        in_specs=(
            (by_row, ids, ids, columns, units, columns, columns, units, rows)
            + (whole, whole, whole, columns, units, rows, whole, whole, whole, by_row)
        ),
        out_specs=(
            (by_row, by_row, columns, units, columns, columns, units, rows)
            + (whole, whole, whole, columns, units, rows, whole, whole, whole)
        ),
        check_vma=False,
    )
```

```python
import math

import jax
import jax.numpy as jnp
from jax import lax
from jax.experimental import pallas as pl
from jax.experimental.pallas import tpu as pltpu
from jax.sharding import PartitionSpec as P

EPSILON = 1e-06
NEG_LARGE = -1e30
LOW = jnp.bfloat16
F32 = jnp.float32
LEN = 512
DIM = 768
HALF = 384
HEADS = 6
STEP = 32
PIECE = 48
LANES = 128
EARLY_ROWS = 6 * PIECE + 6 * (PIECE // 2)
LATE_ROWS = 6 * (PIECE // 2) + 3 * (PIECE // 2) + 9 * (PIECE // 2) + 8
VMEM = pl.BlockSpec(memory_space=pltpu.VMEM)
SMEM = pl.BlockSpec(memory_space=pltpu.SMEM)
ANY = pl.BlockSpec(memory_space=pl.ANY)
FAR = pl.BlockSpec(memory_space=pltpu.HBM)


def nn(left_op, right_op):
    return jnp.dot(left_op, right_op, preferred_element_type=F32)


def nt(left_op, right_op):
    return lax.dot_general(left_op, right_op, (((1,), (1,)), ((), ())), preferred_element_type=F32)


def tn(left_op, right_op):
    return lax.dot_general(left_op, right_op, (((0,), (0,)), ((), ())), preferred_element_type=F32)


def shaped(*shape, kind=F32):
    return jax.ShapeDtypeStruct(shape, kind)


def run(kernel, outs, place, args, scratch=(), spare=8, far=0, after=()):
    after = tuple(jax.tree.leaves(after))
    args = tuple(pltpu.with_memory_space_constraint(arg, pltpu.HBM) for arg in args[:far]) + tuple(args[far:])
    head = () if place is None else (place,)
    in_specs = [SMEM] * len(head) + [FAR] * far + [VMEM] * (len(args) - far) + [ANY] * len(after)
    reads, writes = len(head) + len(args), len(head) + len(args) + len(after)

    def body(*refs):
        kernel(*refs[:reads], *refs[writes:])

    need = sum(math.prod(s.shape) * jnp.dtype(s.dtype).itemsize for s in scratch if s.dtype in (F32, LOW))
    return pl.pallas_call(
        body,
        out_shape=outs,
        in_specs=in_specs,
        out_specs=jax.tree.map(lambda _: VMEM, outs),
        scratch_shapes=scratch,
        name=kernel.__name__,
        compiler_params=pltpu.CompilerParams(vmem_limit_bytes=need + (spare << 20)),
        cost_estimate=pl.CostEstimate(flops=1, bytes_accessed=1, transcendentals=0),
    )(*head, *args, *after)


def over_rows(body, count=LEN // STEP, unroll=LEN // STEP):
    def step(i, carry):
        body(pl.ds(pl.multiple_of(i * STEP, STEP), STEP), i)
        return carry

    lax.fori_loop(0, count, step, 0, unroll=unroll)


def fold(values):
    return jnp.sum(values.reshape(STEP // 8, 8, values.shape[-1]), axis=0)


def fill_bias(seg_row, pad_row, bias):
    spread = jnp.broadcast_to(seg_row[...].astype(F32), (LANES, LEN)).T[:, 0:1]
    for i in range(LEN // STEP):
        down = lax.broadcasted_iota(jnp.int32, (STEP, LEN), 0) + i * STEP
        across = lax.broadcasted_iota(jnp.int32, (STEP, LEN), 1)
        same = (spread[i * STEP : (i + 1) * STEP] == seg_row[...].astype(F32)) & (pad_row[...] == 1)
        bias[i * STEP : (i + 1) * STEP, :] = jnp.where(same | (down == across), 0.0, NEG_LARGE)


def head_of(pair, head):
    lane = lax.broadcasted_iota(jnp.int32, pair.shape, 1)
    return jnp.where((lane < 64) == (head == 0), pair.astype(F32), 0.0)


def attend_kernel(
    tok_far, wq_far, wk_far, wv_far, wo_far, seg_far, pad_far, qb_far, vb_far, ub_far,
    q_ref, k_ref, v_ref, att_ref, lse_ref, part_ref, bias, s_scr, p_scr, tok, wq, wk, wv, wo, seg_row, pad_row, qb, vb, ub, sems,
):
    fars = (tok_far, wq_far, wk_far, wv_far, wo_far, seg_far, pad_far, qb_far, vb_far, ub_far)
    nears = (tok, wq, wk, wv, wo, seg_row, pad_row, qb, vb, ub)
    copies = [pltpu.make_async_copy(far, near, sems.at[j]) for j, (far, near) in enumerate(zip(fars, nears))]
    for j in (5, 6, 0, 1, 7, 2, 3, 8, 4, 9):
        copies[j].start()
    copies[5].wait()
    copies[6].wait()
    fill_bias(seg_row, pad_row, bias)
    copies[0].wait()
    tokens = tok[...]
    copies[1].wait()
    copies[7].wait()
    q_ref[...] = (nn(tokens, wq[...]) + qb[...].reshape(1, HALF)).astype(LOW)
    copies[2].wait()
    k_ref[...] = nn(tokens, wk[...]).astype(LOW)
    copies[3].wait()
    copies[8].wait()
    v_ref[...] = (nn(tokens, wv[...]) + vb[...].reshape(1, HALF)).astype(LOW)

    def pair_step(pair, carry):
        cols = pl.ds(pl.multiple_of(pair * LANES, LANES), LANES)
        outs = []
        lane = lax.broadcasted_iota(jnp.int32, (STEP, LANES), 1)
        for head in range(2):
            s_scr[...] = nt((head_of(q_ref[:, cols], head) * 0.125).astype(LOW), k_ref[:, cols])

            def body(rows, i, head=head):
                scores = s_scr[rows, :] + bias[rows, :]
                peak = jnp.max(scores, axis=-1, keepdims=True)
                grown = jnp.exp(scores - peak)
                total = jnp.sum(grown, axis=-1, keepdims=True)
                p_scr[rows, :] = (grown * (1.0 / total)).astype(LOW)
                lse_ref[rows, :] = jnp.where(lane == 2 * pair + head, peak + jnp.log(total), lse_ref[rows, :])

            over_rows(body)
            outs.append(nn(p_scr[...], v_ref[:, cols]))
        wide = lax.broadcasted_iota(jnp.int32, outs[0].shape, 1)
        att_ref[:, cols] = jnp.where(wide < 64, outs[0], outs[1]).astype(LOW)
        return carry

    lse_ref[...] = jnp.zeros_like(lse_ref)
    lax.fori_loop(0, HEADS // 2, pair_step, 0)
    copies[4].wait()
    copies[9].wait()
    part_ref[:LEN, :] = nn(att_ref[...], wo[...])
    part_ref[LEN:, :] = jnp.zeros((8, DIM), F32)
    for half in range(2):
        part_ref[LEN + half : LEN + half + 1, :] = ub[half * DIM : (half + 1) * DIM].reshape(1, DIM)


def place_pieces(dst, pieces, big, small, offset):
    for source, first, at_big, at_small in each_piece(pieces, big, small, 2 * PIECE):
        dst[rows_at(at_big, at_small, PIECE), :] = source[first + offset : first + offset + PIECE, :].astype(LOW)


def up_kernel(
    place, mine, theirs, tok, ob, g1, s1, wup, *rest
):
    pieces, rest = rest[:10], rest[10:]
    low_ref, zhat_ref, r_ref, act_own, act_oth, dg_own, dg_oth, wup_oth, u_scr, bias = rest
    core, big, small = place[0], place[1], place[2]
    place_pieces(wup_oth.at[core], pieces[:5], big, small, 0)
    place_pieces(wup_oth.at[1 - core], pieces[5:], small, big, 0)

    def norm(rows, i):
        z = tok[rows, :].astype(F32) + (mine[rows, :] + theirs[rows, :]) + ob[...]
        center = z - jnp.mean(z, axis=-1, keepdims=True)
        r = lax.rsqrt(jnp.mean(center * center, axis=-1, keepdims=True) + EPSILON)
        zhat = center * r
        zhat_ref[rows, :] = zhat
        r_ref[rows, :] = r
        low_ref[rows, :] = (zhat * g1[...] + s1[...]).astype(LOW)

    over_rows(norm)
    for half in range(2):
        bias[0:1, half * DIM : (half + 1) * DIM] = mine[LEN + half : LEN + half + 1, :]
        bias[1:2, half * DIM : (half + 1) * DIM] = theirs[LEN + half : LEN + half + 1, :]
    for side in range(2):

        def half_step(half, carry, side=side):
            for chunk in range(3):
                wide = pl.ds(pl.multiple_of(half * DIM + chunk * 256, 256), 256)
                if side == 0:
                    weight, act, dg = wup[:, wide], act_own, dg_own
                else:
                    weight, act, dg = wup_oth[half, :, chunk * 256 : chunk * 256 + 256], act_oth, dg_oth
                u_scr[...] = nn(low_ref[...], weight)

                def gelu(rows, i, act=act, dg=dg, wide=wide):
                    u = u_scr[rows, :] + bias[side : side + 1, wide]
                    cdf = 0.5 + 0.5 * lax.erf(u * (0.5**0.5))
                    act[rows, wide] = (u * cdf).astype(LOW)
                    dg[rows, wide] = cdf + u * (jnp.exp(-0.5 * (u * u)) * 0.3989422804014327)

                over_rows(gelu)
            return carry

        lax.fori_loop(0, 2, half_step, 0)


def down_kernel(
    place, zhat1, g1, s1, act_own, act_oth, wdown, db, g2, s2, cot, *rest
):
    pieces, rest = rest[:10], rest[10:]
    mixed_ref, sgrad_ref, slow_ref, vec_ref, wdown_oth, own_scr, oth_scr, acc = rest
    core, big, small = place[0], place[1], place[2]
    place_pieces(wdown_oth.at[core], pieces[:5], big, small, PIECE)
    place_pieces(wdown_oth.at[1 - core], pieces[5:], small, big, PIECE)
    own_scr[...] = nn(act_own[:, :DIM], wdown[:DIM, :])
    own_scr[...] += nn(act_own[:, DIM:], wdown[DIM:, :])
    oth_scr[...] = nn(act_oth[:, :DIM], wdown_oth[0])
    oth_scr[...] += nn(act_oth[:, DIM:], wdown_oth[1])
    acc[...] = jnp.zeros_like(acc)

    def body(rows, i):
        hidden = zhat1[rows, :] * g1[...] + s1[...]
        z = hidden + (own_scr[rows, :] + oth_scr[rows, :]) + db[...]
        center = z - jnp.mean(z, axis=-1, keepdims=True)
        r = lax.rsqrt(jnp.mean(center * center, axis=-1, keepdims=True) + EPSILON)
        zhat = center * r
        mixed_ref[rows, :] = (zhat * g2[...] + s2[...]).astype(LOW)
        g = cot[rows, :].astype(F32)
        u = g * g2[...]
        grad = r * (u - jnp.mean(u, axis=-1, keepdims=True) - zhat * jnp.mean(u * zhat, axis=-1, keepdims=True))
        sgrad_ref[rows, :] = grad
        slow_ref[rows, :] = grad.astype(LOW)
        acc[0] += fold(grad)
        acc[1] += fold(g * zhat)
        acc[2] += fold(g)

    over_rows(body)
    put_sums(vec_ref, acc, 3)


def put_sums(vec_ref, acc, count):
    vec_ref[...] = jnp.zeros_like(vec_ref)
    for k in range(count):
        vec_ref[k : k + 1, :] = jnp.sum(acc[k], axis=0, keepdims=True)


def each_place(place, keep, send):
    core, big, small = place[0], place[1], place[2]
    for target, half, first, second in ((keep, core, big, small), (send, 1 - core, small, big)):
        for j in range(4):
            for k in range(4):
                yield target, half, 4 * j + k, (first + j) & 3, (second + k) & 3


def rows_at(at_big, at_small, rows):
    return pl.ds(pl.multiple_of(at_big * (4 * rows) + at_small * rows, rows), rows)


def pack(target, start, values):
    rows = values.shape[0]
    for block in range(values.shape[1] // LANES):
        target[start + block * rows : start + (block + 1) * rows, :] = values[:, block * LANES : (block + 1) * LANES]


def early_grad_kernel(place, act_own, slow, low, ug_own, keep, send, downs, ups):
    for half in range(2):
        wide = slice(half * DIM, half * DIM + DIM)
        downs[half] = tn(act_own[:, wide], slow[...])
        ups[half] = tn(low[:, :HALF], ug_own[:, wide])
    for target, half, number, at_big, at_small in each_place(place, keep, send):
        start = number * EARLY_ROWS
        pack(target, start, downs[half, rows_at(at_big, at_small, PIECE), :])
        pack(target, start + 6 * PIECE, ups[half, rows_at(at_big, at_small, PIECE // 2), :])


def unit_kernel(slow, wdown, dg_own, ug_ref, vec_ref, a_scr, acc):
    acc[...] = jnp.zeros_like(acc)
    vec_ref[...] = jnp.zeros_like(vec_ref)
    for half in range(2):
        wide = slice(half * DIM, half * DIM + DIM)
        a_scr[...] = nt(slow[...], wdown[wide, :])

        def body(rows, i, half=half, wide=wide):
            grad = (a_scr[rows, :] * dg_own[rows, wide]).astype(LOW)
            ug_ref[rows, wide] = grad
            acc[half] += fold(grad.astype(F32))

        over_rows(body)
        vec_ref[half : half + 1, :] = jnp.sum(acc[half], axis=0, keepdims=True)


def entry_kernel(
    slow, wdown_oth, dg_oth, wup, wup_oth, ug_own, sgrad, zhat1, r1, g1, att, wo, vec2, vec3,
    first_ref, attg_ref, gwo_ref, vec_ref, a_scr, ug_scr, own_scr, oth_scr, low_scr, acc,
):
    acc[...] = jnp.zeros_like(acc)
    own_scr[...] = nt(ug_own[:, :DIM], wup[:, :DIM])
    own_scr[...] += nt(ug_own[:, DIM:], wup[:, DIM:])
    for half in range(2):
        wide = slice(half * DIM, half * DIM + DIM)
        a_scr[...] = nt(slow[...], wdown_oth[half])

        def body(rows, i, wide=wide):
            ug_scr[rows, :] = (a_scr[rows, :] * dg_oth[rows, wide]).astype(LOW)

        over_rows(body)
        if half == 0:
            oth_scr[...] = nt(ug_scr[...], wup_oth[half])
        else:
            oth_scr[...] += nt(ug_scr[...], wup_oth[half])

    def norm(rows, i):
        g = sgrad[rows, :] + (own_scr[rows, :] + oth_scr[rows, :])
        zhat = zhat1[rows, :]
        u = g * g1[...]
        grad = r1[rows, :] * (u - jnp.mean(u, axis=-1, keepdims=True) - zhat * jnp.mean(u * zhat, axis=-1, keepdims=True))
        first_ref[rows, :] = grad
        low_scr[rows, :] = grad.astype(LOW)
        acc[0] += fold(grad)
        acc[1] += fold(g * zhat)
        acc[2] += fold(g)

    over_rows(norm)
    vec_ref[0:3, :] = vec2[0:3, :]
    for k in range(3):
        vec_ref[3 + k : 4 + k, :] = jnp.sum(acc[k], axis=0, keepdims=True)
    vec_ref[6:8, :] = vec3[0:2, :]
    attg_ref[...] = nt(low_scr[...], wo[...]).astype(LOW)
    gwo_ref[...] = tn(att[...], low_scr[...])


def attend_back_kernel(bias, q, k, v, attg, lse, dq_ref, dk_ref, dv_ref, s_scr, g_scr, p_scr, d_scr, dk_scr, dv_scr):
    def pair_step(pair, carry):
        cols = pl.ds(pl.multiple_of(pair * LANES, LANES), LANES)
        q_turned = q[:, cols].T
        g_turned = attg[:, cols].T
        outs = []
        lane = lax.broadcasted_iota(jnp.int32, (STEP, LANES), 1)
        for head in range(2):
            s_scr[...] = nt((head_of(q[:, cols], head) * 0.125).astype(LOW), k[:, cols])
            g_scr[...] = nt(head_of(attg[:, cols], head).astype(LOW), v[:, cols])

            def body(rows, i, head=head):
                total = jnp.sum(jnp.where(lane == 2 * pair + head, lse[rows, :], 0.0), axis=-1, keepdims=True)
                attention = jnp.exp(s_scr[rows, :] + bias[rows, :] - total)
                grad = g_scr[rows, :]
                p_scr[rows, :] = attention.astype(LOW)
                inner = jnp.sum(grad * attention, axis=-1, keepdims=True)
                d_scr[rows, :] = (attention * (grad - inner)).astype(LOW)

            over_rows(body)
            mine = slice(64 * head, 64 * head + 64)
            outs.append(nn(d_scr[...], k[:, cols]))
            dk_scr[mine, :] = nn(q_turned[mine, :], d_scr[...]) * 0.125
            dv_scr[mine, :] = nn(g_turned[mine, :], p_scr[...])
        wide = lax.broadcasted_iota(jnp.int32, outs[0].shape, 1)
        dq_ref[:, cols] = (jnp.where(wide < 64, outs[0], outs[1]) * 0.125).astype(LOW)
        dk_ref[:, cols] = dk_scr[...].T.astype(LOW)
        dv_ref[:, cols] = dv_scr[...].T.astype(LOW)
        return carry

    lax.fori_loop(0, HEADS // 2, pair_step, 0)


def late_grad_kernel(place, tok, dq, dk, dv, low, ug_own, gwo, vec, keep, send, ups, outs, sums, extra):
    for half in range(2):
        ups[half] = tn(low[:, HALF:], ug_own[:, half * DIM : (half + 1) * DIM])
        outs[half] = gwo[:, half * HALF : (half + 1) * HALF]
    extra[...] = jnp.zeros_like(extra)
    for block in range(DIM // LANES):
        extra[0, block] = vec[:, block * LANES : (block + 1) * LANES]
    turned = tok[...].T
    for number, grads in enumerate((dq, dk, dv)):
        at = slice(number * HALF, number * HALF + HALF)
        total = nn(turned, grads[...])
        sums[0, :, at] = total[:HALF]
        sums[1, :, at] = total[HALF:]
        if number != 1:
            bias_grad = jnp.sum(grads[...].astype(F32), axis=0, keepdims=True)
            for block in range(3):
                row = number // 2 * 3 + block
                extra[0, 6, row : row + 1, :] = bias_grad[:, block * LANES : (block + 1) * LANES]
    for target, half, number, at_big, at_small in each_place(place, keep, send):
        at = rows_at(at_big, at_small, PIECE // 2)
        start = number * LATE_ROWS
        pack(target, start, ups[half, at, :])
        pack(target, start + 3 * PIECE, outs[half, at, :])
        pack(target, start + 9 * (PIECE // 2), sums[half, at, :])
        target[start + LATE_ROWS - 8 : start + LATE_ROWS, :] = extra[half, at_big * 4 + at_small]


def entry_part_kernel(dq, dk, dv, wq, wk, wv, upper, lower):
    for out, rows in ((upper, slice(0, LEN // 2)), (lower, slice(LEN // 2, LEN))):
        out[...] = nt(dq[rows, :], wq[...])
        out[...] += nt(dk[rows, :], wk[...])
        out[...] += nt(dv[rows, :], wv[...])


def total_kernel(first_grad, upper, lower, their_upper, their_lower, out):
    half = LEN // 2
    out[:half, :] = first_grad[:half, :] + (upper[...] + their_upper[...])
    out[half:, :] = first_grad[half:, :] + (lower[...] + their_lower[...])


CROSS = [(0, 3), (3, 0), (1, 2), (2, 1)]


def send_to(value, axis, shift):
    count = 2 if axis in ("w", "c", "t") else 4
    return lax.ppermute(value, axis, [(i, (i + shift) % count) for i in range(count)])


def send_along(value, big, shift):
    pairs = []
    for x in range(4):
        for z in range(4):
            for core in range(2):
                to_x, to_z = ((x + shift) % 4, z) if (core == 0) == big else (x, (z + shift) % 4)
                pairs.append((x * 8 + z * 2 + core, to_x * 8 + to_z * 2 + core))
    return lax.ppermute(value, ("x", "z", "c"), pairs)


def far_kernel(keep, other, right, left):
    half = right.shape[0]
    right[...] = keep[4 * half : 5 * half, :] + other[4 * half : 5 * half, :]
    left[...] = keep[5 * half : 6 * half, :] + other[5 * half : 6 * half, :]


def near_kernel(keep, other, from_left, from_right, right, left, own):
    size = own.shape[0]
    half = size // 2
    own[...] = keep[:size, :] + other[:size, :]
    right[:half, :] = keep[size : size + half, :] + other[size : size + half, :] + from_left[...]
    right[half:, :] = keep[size + half : 2 * size, :] + other[size + half : 2 * size, :]
    left[:half, :] = keep[3 * size : 3 * size + half, :] + other[3 * size : 3 * size + half, :]
    left[half:, :] = keep[3 * size + half :, :] + other[3 * size + half :, :] + from_right[...]


def split_kernel(own, one, two, *outs):
    rows = outs[0].shape[0]
    for j, out in enumerate(outs):
        at = slice(j * rows, (j + 1) * rows)
        out[...] = own[at, :] + one[at, :] + two[at, :]


def piece_kernel(one, two, three, four, out):
    out[...] = (one[...] + two[...]) + (three[...] + four[...])


def twin_kernel(one, two, out):
    out[...] = one[...] + two[...]


def strip_kernel(a, b, c, d, out):
    rows = a.shape[0]
    for j, part in enumerate((a, b, c, d)):
        out[j * rows : (j + 1) * rows, :] = part[...]


def halves_kernel(left, right, top, low):
    half = top.shape[0]
    top[...] = left[:half, :]
    low[...] = right[half:, :]


def tie(*groups):
    flat, tree = jax.tree.flatten(groups)
    return jax.tree.unflatten(tree, lax.optimization_barrier(flat))


class Group:
    def __init__(self, keep=None, send=None):
        self.keep, self.send = keep, send

    def core(self):
        self.other = send_to(self.send, "c", 1)
        return self.send

    def far(self, *after):
        half = self.keep.shape[0] // 8
        right, left = run(far_kernel, (shaped(half, LANES),) * 2, None, (self.keep, self.other), after=after)
        self.far_parts = send_along(right, True, 1), send_along(left, True, -1)
        return left

    def near(self, *after):
        size = self.keep.shape[0] // 4
        parts = (self.keep, self.other) + self.far_parts
        right, left, self.own = run(near_kernel, (shaped(size, LANES),) * 3, None, parts, after=after)
        self.near_parts = send_along(right, True, 1), send_along(left, True, -1)
        return left

    def direct(self, *after):
        rows = self.own.shape[0] // 4
        strips = run(split_kernel, (shaped(rows, LANES),) * 4, None, (self.own,) + self.near_parts, after=after)
        self.strips = (strips[0],) + tuple(send_along(strips[j], False, j if j < 3 else -1) for j in (1, 2, 3))
        return strips[3]

    def pair(self, *after):
        self.piece = run(piece_kernel, shaped(*self.strips[0].shape), None, self.strips, after=after)
        self.twin = send_to(self.piece, "w", 1)
        return self.piece

    def gather_small(self, *after):
        return self.fan_out(run(twin_kernel, shaped(*self.piece.shape), None, (self.piece, self.twin), after=after))

    def fan_out(self, piece):
        self.parts = (piece,) + tuple(send_along(piece, False, shift) for shift in (-1, 2, 1))
        return piece

    def gather_near(self, *after):
        rows, width = self.parts[0].shape
        self.strip = run(strip_kernel, shaped(4 * rows, width), None, self.parts, after=after)
        self.right, self.left = send_along(self.strip, True, -1), send_along(self.strip, True, 1)
        self.their_strip = send_to(self.strip, "c", 1)
        return self.strip

    def gather_far(self, *after):
        half, width = self.strip.shape[0] // 2, self.strip.shape[1]
        top, low = run(halves_kernel, (shaped(half, width),) * 2, None, (self.left, self.right), after=after)
        self.far_top, self.far_low = send_along(top, True, 1), send_along(low, True, -1)
        return low

    def swap_near(self):
        self.their_near = send_to(self.right, "c", 1), send_to(self.left, "c", 1)

    def gather_core(self):
        self.their_far = send_to(self.far_top, "c", 1), send_to(self.far_low, "c", 1)

    def pieces(self):
        mine = (self.strip, self.right, self.left, self.far_top, self.far_low)
        return mine + (self.their_strip,) + self.their_near + self.their_far


def each_piece(pieces, big, small, rows):
    own, right, left, far_top, far_low = pieces
    for turn, source, start, count in ((0, own, 0, 4), (1, right, 0, 4), (3, left, 0, 4), (2, far_top, 0, 2), (2, far_low, 2, 2)):
        for j in range(count):
            yield source, j * rows, (big + turn) & 3, (small + start + j) & 3


def unpack(target, rows, column, source, start, count, blocks):
    for block in range(blocks):
        at = column + block * LANES
        at = slice(at, at + LANES) if isinstance(at, int) else pl.ds(pl.multiple_of(at, LANES), LANES)
        target[rows, at] = source[start + block * count : start + (block + 1) * count, :]


def early_out_kernel(place, *refs):
    pieces, (down, up) = refs[:10], refs[10:]
    core, big, small = place[0], place[1], place[2]
    for side, half, along, across in ((pieces[:5], core, big, small), (pieces[5:], 1 - core, small, big)):
        for source, first, at_big, at_small in each_piece(side, along, across, EARLY_ROWS):
            unpack(down.at[half], rows_at(at_big, at_small, PIECE), 0, source, first, PIECE, 6)
            unpack(up, rows_at(at_big, at_small, PIECE // 2), half * DIM, source, first + 6 * PIECE, PIECE // 2, 6)


def late_out_kernel(place, up_early, *refs):
    pieces, (up, out_wo, qw, kw, vw, vec, biases, tiles) = refs[:10], refs[10:]
    core, big, small = place[0], place[1], place[2]
    count = PIECE // 2
    up[:HALF, :] = up_early[...]
    for side, half, along, across in ((pieces[:5], core, big, small), (pieces[5:], 1 - core, small, big)):
        for source, first, at_big, at_small in each_piece(side, along, across, LATE_ROWS):
            row = at_big * (4 * count) + at_small * count
            rows = pl.ds(pl.multiple_of(HALF + row, count), count)
            unpack(up, rows, half * DIM, source, first, count, 6)
            unpack(out_wo, rows_at(at_big, at_small, count), half * HALF, source, first + 6 * count, count, 3)
            rows = pl.ds(pl.multiple_of(half * HALF + row, count), count)
            for number, out in enumerate((qw, kw, vw)):
                unpack(out, rows, 0, source, first + (9 + 3 * number) * count, count, 3)
            tiles[half, at_big * 4 + at_small] = source[first + LATE_ROWS - 8 : first + LATE_ROWS, :]
    for block in range(DIM // LANES):
        vec[:, block * LANES : (block + 1) * LANES] = tiles[0, block]
    biases[...] = tiles[0, 6]


def on_device(
    tokens,
    seg_ids,
    pad_mask,
    query_weight,
    query_bias,
    key_weight,
    value_weight,
    value_bias,
    out_weight,
    out_bias,
    first_gain,
    first_shift,
    up_weight,
    up_bias,
    down_weight,
    down_bias,
    second_gain,
    second_shift,
    cotangent,
):
    tok = tokens.reshape(LEN, DIM)
    cot = cotangent.reshape(LEN, DIM)
    at_x, at_z, at_c = (lax.axis_index(name) for name in ("x", "z", "c"))
    at_big, at_small = jnp.where(at_c == 0, at_x, at_z), jnp.where(at_c == 0, at_z, at_x)
    place = jnp.stack([at_c, at_big, at_small]).astype(jnp.int32)
    row = lambda vector: vector.reshape(1, -1)
    ob, g1, s1, db, g2, s2 = (row(v) for v in (out_bias, first_gain, first_shift, down_bias, second_gain, second_shift))
    mat = lambda *shape: pltpu.VMEM(shape, F32)
    low_mat = lambda *shape: pltpu.VMEM(shape, LOW)

    first = (at_big * 4 + at_small) * PIECE
    up_shard = lax.dynamic_slice(up_weight, (first, at_c * DIM), (PIECE, DIM))
    down_shard = lax.dynamic_slice(down_weight, (at_c * DIM + first, 0), (PIECE, DIM))
    shard = lax.ppermute(jnp.concatenate([up_shard, down_shard]).astype(F32), ("w", "t"), CROSS)
    fetch = Group()
    q, k, v, att, lse, part, bias = run(
        attend_kernel,
        (shaped(LEN, HALF, kind=LOW),) * 4 + (shaped(LEN, 128), shaped(LEN + 8, DIM), shaped(LEN, LEN)),
        None,
        (tok, query_weight, key_weight, value_weight, out_weight, seg_ids, pad_mask, query_bias, value_bias, up_bias),
        [mat(LEN, LEN), low_mat(LEN, LEN), low_mat(LEN, DIM)]
        + [low_mat(DIM, HALF)] * 3
        + [low_mat(HALF, DIM), pltpu.VMEM((1, LEN), jnp.int32), pltpu.VMEM((1, LEN), jnp.int32)]
        + [mat(HALF), mat(HALF), mat(2 * DIM), pltpu.SemaphoreType.DMA((10,))],
        far=10,
    )
    part_other = send_to(part, "t", 1)
    part, shard = tie(part, shard)
    fetch.fan_out(shard)
    fetch.gather_near()
    fetch.gather_far()
    fetch.swap_near()
    fetch.gather_core()
    low, zhat1, r1, act_own, act_oth, dg_own, dg_oth, wup_oth = run(
        up_kernel,
        (
            shaped(LEN, DIM, kind=LOW),
            shaped(LEN, DIM),
            shaped(LEN, 1),
            shaped(LEN, 2 * DIM, kind=LOW),
            shaped(LEN, 2 * DIM, kind=LOW),
            shaped(LEN, 2 * DIM),
            shaped(LEN, 2 * DIM),
            shaped(2, DIM, DIM, kind=LOW),
        ),
        place,
        (part, part_other, tok, ob, g1, s1, up_weight) + fetch.pieces(),
        [mat(LEN, 256), mat(8, 2 * DIM)],
    )
    mixed, sgrad, slow, vec2, wdown_oth = run(
        down_kernel,
        (shaped(LEN, DIM, kind=LOW), shaped(LEN, DIM), shaped(LEN, DIM, kind=LOW), shaped(8, DIM), shaped(2, DIM, DIM, kind=LOW)),
        place,
        (zhat1, g1, s1, act_own, act_oth, down_weight, db, g2, s2, cot) + fetch.pieces(),
        [mat(LEN, DIM), mat(LEN, DIM), mat(3, 8, DIM)],
    )
    ug_own, vec3 = run(
        unit_kernel,
        (shaped(LEN, 2 * DIM, kind=LOW), shaped(8, DIM)),
        None,
        (slow, down_weight, dg_own),
        [mat(LEN, DIM), mat(2, 8, DIM)],
    )
    keep, send = run(
        early_grad_kernel,
        (shaped(16 * EARLY_ROWS, LANES),) * 2,
        place,
        (act_own, slow, low, ug_own),
        [mat(2, DIM, DIM), mat(2, HALF, DIM)],
    )
    early = Group(keep, send)
    after = early.core()
    first_grad, attg, gwo, vec = run(
        entry_kernel,
        (shaped(LEN, DIM), shaped(LEN, HALF, kind=LOW), shaped(HALF, DIM), shaped(8, DIM)),
        None,
        (slow, wdown_oth, dg_oth, up_weight, wup_oth, ug_own, sgrad, zhat1, r1, g1, att, out_weight, vec2, vec3),
        [mat(LEN, DIM), low_mat(LEN, DIM), mat(LEN, DIM), mat(LEN, DIM), low_mat(LEN, DIM), mat(3, 8, DIM)],
        after=after,
    )
    after = early.far(vec)
    dq, dk, dv = run(
        attend_back_kernel,
        (shaped(LEN, HALF, kind=LOW),) * 3,
        None,
        (bias, q, k, v, attg, lse),
        [mat(LEN, LEN), mat(LEN, LEN), low_mat(LEN, LEN), low_mat(LEN, LEN), mat(128, LEN), mat(128, LEN)],
        after=after,
    )
    after = early.near(dq)
    keep, send = run(
        late_grad_kernel,
        (shaped(16 * LATE_ROWS, LANES),) * 2,
        place,
        (tok, dq, dk, dv, low, ug_own, gwo, vec),
        [mat(2, HALF, DIM), mat(2, HALF, HALF), mat(2, HALF, 3 * HALF), mat(2, 16, 8, LANES)],
        after=after,
    )
    late = Group(keep, send)
    late.core()
    upper, lower = run(
        entry_part_kernel, (shaped(LEN // 2, DIM),) * 2, None, (dq, dk, dv, query_weight, key_weight, value_weight), after=keep
    )
    their_upper = send_to(upper, "t", 1)
    early.near_parts, late.other = tie(early.near_parts, late.other)
    early.direct()
    late.far()
    early.strips, late.far_parts, their_upper = tie(early.strips, late.far_parts, their_upper)
    early.pair()
    late.near()
    early.twin, late.near_parts = tie(early.twin, late.near_parts)
    early.gather_small()
    late.direct()
    early.parts, late.strips = tie(early.parts, late.strips)
    early.gather_near()
    late.pair()
    early.right, early.left, early.their_strip, late.twin = tie(early.right, early.left, early.their_strip, late.twin)
    early.gather_far()
    late.gather_small()
    early.right, early.left, early.far_top, early.far_low, late.parts, lower = tie(
        early.right, early.left, early.far_top, early.far_low, late.parts, lower
    )
    their_lower = send_to(lower, "t", 1)
    early.swap_near()
    early.gather_core()
    late.gather_near()
    down_sum, up_early = run(early_out_kernel, (shaped(2, DIM, DIM), shaped(HALF, 2 * DIM)), place, early.pieces(), spare=14)
    late.right, late.left, late.their_strip, up_early = tie(late.right, late.left, late.their_strip, up_early)
    late.gather_far()
    late.swap_near()
    late.far_top, late.far_low, their_lower = tie(late.far_top, late.far_low, their_lower)
    input_gradient = run(total_kernel, shaped(LEN, DIM), None, (first_grad, upper, lower, their_upper, their_lower))
    late.gather_core()
    weight = shaped(DIM, HALF)
    up_sum, ow, qw, kw, vw, vec, biases = run(
        late_out_kernel,
        (shaped(DIM, 2 * DIM), shaped(HALF, DIM), weight, weight, weight, shaped(8, DIM), shaped(8, LANES)),
        place,
        (up_early,) + late.pieces(),
        [mat(2, 16, 8, LANES)],
        spare=18,
        after=input_gradient,
    )
    db, sg, ss, ob, fg, fs = (vec[j] for j in range(6))
    return (
        mixed.reshape(1, LEN, DIM),
        input_gradient.reshape(1, LEN, DIM),
        qw,
        biases[0:3].reshape(HALF),
        kw,
        vw,
        biases[3:6].reshape(HALF),
        ow,
        ob,
        fg,
        fs,
        up_sum,
        vec[6:8].reshape(2 * DIM),
        down_sum.reshape(2 * DIM, DIM),
        db,
        sg,
        ss,
    )


ROWS_AXES = ("x", "w", "z", "c")


def solution(mesh):
    fine = jax.sharding.Mesh(mesh.devices.reshape(4, 2, 4, 2, 2), ROWS_AXES + ("t",))
    by_row, ids = P(ROWS_AXES, None, None), P(ROWS_AXES, None)
    columns, units, rows, whole = P(None, "t"), P("t"), P("t", None), P()
    return jax.shard_map(
        on_device,
        mesh=fine,
        in_specs=(
            (by_row, ids, ids, columns, units, columns, columns, units, rows)
            + (whole, whole, whole, columns, units, rows, whole, whole, whole, by_row)
        ),
        out_specs=(
            (by_row, by_row, columns, units, columns, columns, units, rows)
            + (whole, whole, whole, columns, units, rows, whole, whole, whole)
        ),
        check_vma=False,
    )
```

```python
import math

import jax
import jax.numpy as jnp
from jax import lax
from jax.experimental import pallas as pl
from jax.experimental.pallas import tpu as pltpu
from jax.sharding import PartitionSpec as P

EPSILON = 1e-06
NEG_LARGE = -1e30
LOW = jnp.bfloat16
F32 = jnp.float32
LEN = 512
DIM = 768
HALF = 384
HEADS = 6
STEP = 32
PIECE = 48
LANES = 128
EARLY_ROWS = 6 * PIECE + 6 * (PIECE // 2)
LATE_ROWS = 6 * (PIECE // 2) + 3 * (PIECE // 2) + 9 * (PIECE // 2) + 8
VMEM = pl.BlockSpec(memory_space=pltpu.VMEM)
SMEM = pl.BlockSpec(memory_space=pltpu.SMEM)
ANY = pl.BlockSpec(memory_space=pl.ANY)
FAR = pl.BlockSpec(memory_space=pltpu.HBM)


def nn(left_op, right_op):
    return jnp.dot(left_op, right_op, preferred_element_type=F32)


def nt(left_op, right_op):
    return lax.dot_general(left_op, right_op, (((1,), (1,)), ((), ())), preferred_element_type=F32)


def tn(left_op, right_op):
    return lax.dot_general(left_op, right_op, (((0,), (0,)), ((), ())), preferred_element_type=F32)


def shaped(*shape, kind=F32):
    return jax.ShapeDtypeStruct(shape, kind)


def run(kernel, outs, place, args, scratch=(), spare=8, far=0, after=()):
    after = tuple(jax.tree.leaves(after))
    args = tuple(pltpu.with_memory_space_constraint(arg, pltpu.HBM) for arg in args[:far]) + tuple(args[far:])
    head = () if place is None else (place,)
    in_specs = [SMEM] * len(head) + [FAR] * far + [VMEM] * (len(args) - far) + [ANY] * len(after)
    reads, writes = len(head) + len(args), len(head) + len(args) + len(after)

    def body(*refs):
        kernel(*refs[:reads], *refs[writes:])

    need = sum(math.prod(s.shape) * jnp.dtype(s.dtype).itemsize for s in scratch if s.dtype in (F32, LOW))
    return pl.pallas_call(
        body,
        out_shape=outs,
        in_specs=in_specs,
        out_specs=jax.tree.map(lambda _: VMEM, outs),
        scratch_shapes=scratch,
        name=kernel.__name__,
        compiler_params=pltpu.CompilerParams(vmem_limit_bytes=need + (spare << 20)),
        cost_estimate=pl.CostEstimate(flops=1, bytes_accessed=1, transcendentals=0),
    )(*head, *args, *after)


def over_rows(body, count=LEN // STEP, unroll=LEN // STEP):
    def step(i, carry):
        body(pl.ds(pl.multiple_of(i * STEP, STEP), STEP), i)
        return carry

    lax.fori_loop(0, count, step, 0, unroll=unroll)


def fold(values):
    return jnp.sum(values.reshape(STEP // 8, 8, values.shape[-1]), axis=0)


def fill_bias(seg_row, pad_row, bias):
    spread = jnp.broadcast_to(seg_row[...].astype(F32), (LANES, LEN)).T[:, 0:1]
    for i in range(LEN // STEP):
        down = lax.broadcasted_iota(jnp.int32, (STEP, LEN), 0) + i * STEP
        across = lax.broadcasted_iota(jnp.int32, (STEP, LEN), 1)
        same = (spread[i * STEP : (i + 1) * STEP] == seg_row[...].astype(F32)) & (pad_row[...] == 1)
        bias[i * STEP : (i + 1) * STEP, :] = jnp.where(same | (down == across), 0.0, NEG_LARGE)


def head_of(pair, head):
    lane = lax.broadcasted_iota(jnp.int32, pair.shape, 1)
    return jnp.where((lane < 64) == (head == 0), pair.astype(F32), 0.0)


def attend_kernel(
    tok_far, wq_far, wk_far, wv_far, wo_far, seg_far, pad_far, qb_far, vb_far, ub_far,
    q_ref, k_ref, v_ref, att_ref, lse_ref, part_ref, bias, s_scr, p_scr, tok, wq, wk, wv, wo, seg_row, pad_row, qb, vb, ub, sems,
):
    fars = (tok_far, wq_far, wk_far, wv_far, wo_far, seg_far, pad_far, qb_far, vb_far, ub_far)
    nears = (tok, wq, wk, wv, wo, seg_row, pad_row, qb, vb, ub)
    copies = [pltpu.make_async_copy(far, near, sems.at[j]) for j, (far, near) in enumerate(zip(fars, nears))]
    for j in (5, 6, 0, 1, 7, 2, 3, 8, 4, 9):
        copies[j].start()
    copies[5].wait()
    copies[6].wait()
    fill_bias(seg_row, pad_row, bias)
    copies[0].wait()
    tokens = tok[...]
    copies[1].wait()
    copies[7].wait()
    q_ref[...] = (nn(tokens, wq[...]) + qb[...].reshape(1, HALF)).astype(LOW)
    copies[2].wait()
    k_ref[...] = nn(tokens, wk[...]).astype(LOW)
    copies[3].wait()
    copies[8].wait()
    v_ref[...] = (nn(tokens, wv[...]) + vb[...].reshape(1, HALF)).astype(LOW)

    def pair_step(pair, carry):
        cols = pl.ds(pl.multiple_of(pair * LANES, LANES), LANES)
        outs = []
        lane = lax.broadcasted_iota(jnp.int32, (STEP, LANES), 1)
        for head in range(2):
            s_scr[...] = nt((head_of(q_ref[:, cols], head) * 0.125).astype(LOW), k_ref[:, cols])

            def body(rows, i, head=head):
                scores = s_scr[rows, :] + bias[rows, :]
                peak = jnp.max(scores, axis=-1, keepdims=True)
                grown = jnp.exp(scores - peak)
                total = jnp.sum(grown, axis=-1, keepdims=True)
                p_scr[rows, :] = (grown * (1.0 / total)).astype(LOW)
                lse_ref[rows, :] = jnp.where(lane == 2 * pair + head, peak + jnp.log(total), lse_ref[rows, :])

            over_rows(body)
            outs.append(nn(p_scr[...], v_ref[:, cols]))
        wide = lax.broadcasted_iota(jnp.int32, outs[0].shape, 1)
        att_ref[:, cols] = jnp.where(wide < 64, outs[0], outs[1]).astype(LOW)
        return carry

    lse_ref[...] = jnp.zeros_like(lse_ref)
    lax.fori_loop(0, HEADS // 2, pair_step, 0)
    copies[4].wait()
    copies[9].wait()
    part_ref[:LEN, :] = nn(att_ref[...], wo[...])
    part_ref[LEN:, :] = jnp.zeros((8, DIM), F32)
    for half in range(2):
        part_ref[LEN + half : LEN + half + 1, :] = ub[half * DIM : (half + 1) * DIM].reshape(1, DIM)


def place_pieces(dst, pieces, big, small, offset):
    for source, first, at_big, at_small in each_piece(pieces, big, small, 2 * PIECE):
        dst[rows_at(at_big, at_small, PIECE), :] = source[first + offset : first + offset + PIECE, :].astype(LOW)


def up_kernel(
    place, mine, theirs, tok, ob, g1, s1, wup, *rest
):
    pieces, rest = rest[:10], rest[10:]
    low_ref, zhat_ref, r_ref, act_own, act_oth, dg_own, dg_oth, wup_oth, u_scr, bias = rest
    core, big, small = place[0], place[1], place[2]
    place_pieces(wup_oth.at[core], pieces[:5], big, small, 0)
    place_pieces(wup_oth.at[1 - core], pieces[5:], small, big, 0)

    def norm(rows, i):
        z = tok[rows, :].astype(F32) + (mine[rows, :] + theirs[rows, :]) + ob[...]
        center = z - jnp.mean(z, axis=-1, keepdims=True)
        r = lax.rsqrt(jnp.mean(center * center, axis=-1, keepdims=True) + EPSILON)
        zhat = center * r
        zhat_ref[rows, :] = zhat
        r_ref[rows, :] = r
        low_ref[rows, :] = (zhat * g1[...] + s1[...]).astype(LOW)

    over_rows(norm)
    for half in range(2):
        bias[0:1, half * DIM : (half + 1) * DIM] = mine[LEN + half : LEN + half + 1, :]
        bias[1:2, half * DIM : (half + 1) * DIM] = theirs[LEN + half : LEN + half + 1, :]
    for side in range(2):

        def half_step(half, carry, side=side):
            for chunk in range(3):
                wide = pl.ds(pl.multiple_of(half * DIM + chunk * 256, 256), 256)
                if side == 0:
                    weight, act, dg = wup[:, wide], act_own, dg_own
                else:
                    weight, act, dg = wup_oth[half, :, chunk * 256 : chunk * 256 + 256], act_oth, dg_oth
                u_scr[...] = nn(low_ref[...], weight)

                def gelu(rows, i, act=act, dg=dg, wide=wide):
                    u = u_scr[rows, :] + bias[side : side + 1, wide]
                    cdf = 0.5 + 0.5 * lax.erf(u * (0.5**0.5))
                    act[rows, wide] = (u * cdf).astype(LOW)
                    dg[rows, wide] = cdf + u * (jnp.exp(-0.5 * (u * u)) * 0.3989422804014327)

                over_rows(gelu)
            return carry

        lax.fori_loop(0, 2, half_step, 0)


def down_kernel(
    place, zhat1, g1, s1, act_own, act_oth, wdown, db, g2, s2, cot, *rest
):
    pieces, rest = rest[:10], rest[10:]
    mixed_ref, sgrad_ref, slow_ref, vec_ref, wdown_oth, own_scr, oth_scr, acc = rest
    core, big, small = place[0], place[1], place[2]
    place_pieces(wdown_oth.at[core], pieces[:5], big, small, PIECE)
    place_pieces(wdown_oth.at[1 - core], pieces[5:], small, big, PIECE)
    own_scr[...] = nn(act_own[:, :DIM], wdown[:DIM, :])
    own_scr[...] += nn(act_own[:, DIM:], wdown[DIM:, :])
    oth_scr[...] = nn(act_oth[:, :DIM], wdown_oth[0])
    oth_scr[...] += nn(act_oth[:, DIM:], wdown_oth[1])
    acc[...] = jnp.zeros_like(acc)

    def body(rows, i):
        hidden = zhat1[rows, :] * g1[...] + s1[...]
        z = hidden + (own_scr[rows, :] + oth_scr[rows, :]) + db[...]
        center = z - jnp.mean(z, axis=-1, keepdims=True)
        r = lax.rsqrt(jnp.mean(center * center, axis=-1, keepdims=True) + EPSILON)
        zhat = center * r
        mixed_ref[rows, :] = (zhat * g2[...] + s2[...]).astype(LOW)
        g = cot[rows, :].astype(F32)
        u = g * g2[...]
        grad = r * (u - jnp.mean(u, axis=-1, keepdims=True) - zhat * jnp.mean(u * zhat, axis=-1, keepdims=True))
        sgrad_ref[rows, :] = grad
        slow_ref[rows, :] = grad.astype(LOW)
        acc[0] += fold(grad)
        acc[1] += fold(g * zhat)
        acc[2] += fold(g)

    over_rows(body)
    put_sums(vec_ref, acc, 3)


def put_sums(vec_ref, acc, count):
    vec_ref[...] = jnp.zeros_like(vec_ref)
    for k in range(count):
        vec_ref[k : k + 1, :] = jnp.sum(acc[k], axis=0, keepdims=True)


def each_place(place, keep, send):
    core, big, small = place[0], place[1], place[2]
    for target, half, first, second in ((keep, core, big, small), (send, 1 - core, small, big)):
        for j in range(4):
            for k in range(4):
                yield target, half, 4 * j + k, (first + j) & 3, (second + k) & 3


def rows_at(at_big, at_small, rows):
    return pl.ds(pl.multiple_of(at_big * (4 * rows) + at_small * rows, rows), rows)


def pack(target, start, values):
    rows = values.shape[0]
    for block in range(values.shape[1] // LANES):
        target[start + block * rows : start + (block + 1) * rows, :] = values[:, block * LANES : (block + 1) * LANES]


def early_grad_kernel(place, act_own, slow, low, ug_own, keep, send, downs, ups):
    for half in range(2):
        wide = slice(half * DIM, half * DIM + DIM)
        downs[half] = tn(act_own[:, wide], slow[...])
        ups[half] = tn(low[:, :HALF], ug_own[:, wide])
    for target, half, number, at_big, at_small in each_place(place, keep, send):
        start = number * EARLY_ROWS
        pack(target, start, downs[half, rows_at(at_big, at_small, PIECE), :])
        pack(target, start + 6 * PIECE, ups[half, rows_at(at_big, at_small, PIECE // 2), :])


def unit_kernel(slow, wdown, dg_own, ug_ref, vec_ref, a_scr, acc):
    acc[...] = jnp.zeros_like(acc)
    vec_ref[...] = jnp.zeros_like(vec_ref)
    for half in range(2):
        wide = slice(half * DIM, half * DIM + DIM)
        a_scr[...] = nt(slow[...], wdown[wide, :])

        def body(rows, i, half=half, wide=wide):
            grad = (a_scr[rows, :] * dg_own[rows, wide]).astype(LOW)
            ug_ref[rows, wide] = grad
            acc[half] += fold(grad.astype(F32))

        over_rows(body)
        vec_ref[half : half + 1, :] = jnp.sum(acc[half], axis=0, keepdims=True)


def entry_kernel(
    slow, wdown_oth, dg_oth, wup, wup_oth, ug_own, sgrad, zhat1, r1, g1, att, wo, vec2, vec3,
    first_ref, attg_ref, gwo_ref, vec_ref, a_scr, ug_scr, own_scr, oth_scr, low_scr, acc,
):
    acc[...] = jnp.zeros_like(acc)
    own_scr[...] = nt(ug_own[:, :DIM], wup[:, :DIM])
    own_scr[...] += nt(ug_own[:, DIM:], wup[:, DIM:])
    for half in range(2):
        wide = slice(half * DIM, half * DIM + DIM)
        a_scr[...] = nt(slow[...], wdown_oth[half])

        def body(rows, i, wide=wide):
            ug_scr[rows, :] = (a_scr[rows, :] * dg_oth[rows, wide]).astype(LOW)

        over_rows(body)
        if half == 0:
            oth_scr[...] = nt(ug_scr[...], wup_oth[half])
        else:
            oth_scr[...] += nt(ug_scr[...], wup_oth[half])

    def norm(rows, i):
        g = sgrad[rows, :] + (own_scr[rows, :] + oth_scr[rows, :])
        zhat = zhat1[rows, :]
        u = g * g1[...]
        grad = r1[rows, :] * (u - jnp.mean(u, axis=-1, keepdims=True) - zhat * jnp.mean(u * zhat, axis=-1, keepdims=True))
        first_ref[rows, :] = grad
        low_scr[rows, :] = grad.astype(LOW)
        acc[0] += fold(grad)
        acc[1] += fold(g * zhat)
        acc[2] += fold(g)

    over_rows(norm)
    vec_ref[0:3, :] = vec2[0:3, :]
    for k in range(3):
        vec_ref[3 + k : 4 + k, :] = jnp.sum(acc[k], axis=0, keepdims=True)
    vec_ref[6:8, :] = vec3[0:2, :]
    attg_ref[...] = nt(low_scr[...], wo[...]).astype(LOW)
    gwo_ref[...] = tn(att[...], low_scr[...])


def attend_back_kernel(bias, q, k, v, attg, lse, dq_ref, dk_ref, dv_ref, s_scr, g_scr, p_scr, d_scr, dk_scr, dv_scr):
    def pair_step(pair, carry):
        cols = pl.ds(pl.multiple_of(pair * LANES, LANES), LANES)
        q_turned = q[:, cols].T
        g_turned = attg[:, cols].T
        outs = []
        lane = lax.broadcasted_iota(jnp.int32, (STEP, LANES), 1)
        for head in range(2):
            s_scr[...] = nt((head_of(q[:, cols], head) * 0.125).astype(LOW), k[:, cols])
            g_scr[...] = nt(head_of(attg[:, cols], head).astype(LOW), v[:, cols])

            def body(rows, i, head=head):
                total = jnp.sum(jnp.where(lane == 2 * pair + head, lse[rows, :], 0.0), axis=-1, keepdims=True)
                attention = jnp.exp(s_scr[rows, :] + bias[rows, :] - total)
                grad = g_scr[rows, :]
                p_scr[rows, :] = attention.astype(LOW)
                inner = jnp.sum(grad * attention, axis=-1, keepdims=True)
                d_scr[rows, :] = (attention * (grad - inner)).astype(LOW)

            over_rows(body)
            mine = slice(64 * head, 64 * head + 64)
            outs.append(nn(d_scr[...], k[:, cols]))
            dk_scr[mine, :] = nn(q_turned[mine, :], d_scr[...]) * 0.125
            dv_scr[mine, :] = nn(g_turned[mine, :], p_scr[...])
        wide = lax.broadcasted_iota(jnp.int32, outs[0].shape, 1)
        dq_ref[:, cols] = (jnp.where(wide < 64, outs[0], outs[1]) * 0.125).astype(LOW)
        dk_ref[:, cols] = dk_scr[...].T.astype(LOW)
        dv_ref[:, cols] = dv_scr[...].T.astype(LOW)
        return carry

    lax.fori_loop(0, HEADS // 2, pair_step, 0)


def late_grad_kernel(place, tok, dq, dk, dv, low, ug_own, gwo, vec, keep, send, ups, outs, sums, extra):
    for half in range(2):
        ups[half] = tn(low[:, HALF:], ug_own[:, half * DIM : (half + 1) * DIM])
        outs[half] = gwo[:, half * HALF : (half + 1) * HALF]
    extra[...] = jnp.zeros_like(extra)
    for block in range(DIM // LANES):
        extra[0, block] = vec[:, block * LANES : (block + 1) * LANES]
    turned = tok[...].T
    for number, grads in enumerate((dq, dk, dv)):
        at = slice(number * HALF, number * HALF + HALF)
        total = nn(turned, grads[...])
        sums[0, :, at] = total[:HALF]
        sums[1, :, at] = total[HALF:]
        if number != 1:
            bias_grad = jnp.sum(grads[...].astype(F32), axis=0, keepdims=True)
            for block in range(3):
                row = number // 2 * 3 + block
                extra[0, 6, row : row + 1, :] = bias_grad[:, block * LANES : (block + 1) * LANES]
    for target, half, number, at_big, at_small in each_place(place, keep, send):
        at = rows_at(at_big, at_small, PIECE // 2)
        start = number * LATE_ROWS
        pack(target, start, ups[half, at, :])
        pack(target, start + 3 * PIECE, outs[half, at, :])
        pack(target, start + 9 * (PIECE // 2), sums[half, at, :])
        target[start + LATE_ROWS - 8 : start + LATE_ROWS, :] = extra[half, at_big * 4 + at_small]


def entry_part_kernel(dq, dk, dv, wq, wk, wv, upper, lower):
    for out, rows in ((upper, slice(0, LEN // 2)), (lower, slice(LEN // 2, LEN))):
        out[...] = nt(dq[rows, :], wq[...])
        out[...] += nt(dk[rows, :], wk[...])
        out[...] += nt(dv[rows, :], wv[...])


def total_kernel(first_grad, upper, lower, their_upper, their_lower, out):
    half = LEN // 2
    out[:half, :] = first_grad[:half, :] + (upper[...] + their_upper[...])
    out[half:, :] = first_grad[half:, :] + (lower[...] + their_lower[...])


CROSS = [(0, 3), (3, 0), (1, 2), (2, 1)]


def send_to(value, axis, shift):
    count = 2 if axis in ("w", "c", "t") else 4
    return lax.ppermute(value, axis, [(i, (i + shift) % count) for i in range(count)])


def send_along(value, big, shift):
    pairs = []
    for x in range(4):
        for z in range(4):
            for core in range(2):
                to_x, to_z = ((x + shift) % 4, z) if (core == 0) == big else (x, (z + shift) % 4)
                pairs.append((x * 8 + z * 2 + core, to_x * 8 + to_z * 2 + core))
    return lax.ppermute(value, ("x", "z", "c"), pairs)


def far_kernel(keep, other, right, left):
    half = right.shape[0]
    right[...] = keep[4 * half : 5 * half, :] + other[4 * half : 5 * half, :]
    left[...] = keep[5 * half : 6 * half, :] + other[5 * half : 6 * half, :]


def near_kernel(keep, other, from_left, from_right, right, left, own):
    size = own.shape[0]
    half = size // 2
    own[...] = keep[:size, :] + other[:size, :]
    right[:half, :] = keep[size : size + half, :] + other[size : size + half, :] + from_left[...]
    right[half:, :] = keep[size + half : 2 * size, :] + other[size + half : 2 * size, :]
    left[:half, :] = keep[3 * size : 3 * size + half, :] + other[3 * size : 3 * size + half, :]
    left[half:, :] = keep[3 * size + half :, :] + other[3 * size + half :, :] + from_right[...]


def split_kernel(own, one, two, *outs):
    rows = outs[0].shape[0]
    for j, out in enumerate(outs):
        at = slice(j * rows, (j + 1) * rows)
        out[...] = own[at, :] + one[at, :] + two[at, :]


def piece_kernel(one, two, three, four, out):
    out[...] = (one[...] + two[...]) + (three[...] + four[...])


def twin_kernel(one, two, out):
    out[...] = one[...] + two[...]


def strip_kernel(a, b, c, d, out):
    rows = a.shape[0]
    for j, part in enumerate((a, b, c, d)):
        out[j * rows : (j + 1) * rows, :] = part[...]


def halves_kernel(left, right, top, low):
    half = top.shape[0]
    top[...] = left[:half, :]
    low[...] = right[half:, :]


def tie(*groups):
    flat, tree = jax.tree.flatten(groups)
    return jax.tree.unflatten(tree, lax.optimization_barrier(flat))


class Group:
    def __init__(self, keep=None, send=None):
        self.keep, self.send = keep, send

    def core(self):
        self.other = send_to(self.send, "c", 1)
        return self.send

    def far(self, *after):
        half = self.keep.shape[0] // 8
        right, left = run(far_kernel, (shaped(half, LANES),) * 2, None, (self.keep, self.other), after=after)
        self.far_parts = send_along(right, True, 1), send_along(left, True, -1)
        return left

    def near(self, *after):
        size = self.keep.shape[0] // 4
        parts = (self.keep, self.other) + self.far_parts
        right, left, self.own = run(near_kernel, (shaped(size, LANES),) * 3, None, parts, after=after)
        self.near_parts = send_along(right, True, 1), send_along(left, True, -1)
        return left

    def direct(self, *after):
        rows = self.own.shape[0] // 4
        strips = run(split_kernel, (shaped(rows, LANES),) * 4, None, (self.own,) + self.near_parts, after=after)
        self.strips = (strips[0],) + tuple(send_along(strips[j], False, j if j < 3 else -1) for j in (1, 2, 3))
        return strips[3]

    def pair(self, *after):
        self.piece = run(piece_kernel, shaped(*self.strips[0].shape), None, self.strips, after=after)
        self.twin = send_to(self.piece, "w", 1)
        return self.piece

    def gather_small(self, *after):
        return self.fan_out(run(twin_kernel, shaped(*self.piece.shape), None, (self.piece, self.twin), after=after))

    def fan_out(self, piece):
        self.parts = (piece,) + tuple(send_along(piece, False, shift) for shift in (-1, 2, 1))
        return piece

    def gather_near(self, *after):
        rows, width = self.parts[0].shape
        self.strip = run(strip_kernel, shaped(4 * rows, width), None, self.parts, after=after)
        self.right, self.left = send_along(self.strip, True, -1), send_along(self.strip, True, 1)
        self.their_strip = send_to(self.strip, "c", 1)
        return self.strip

    def gather_far(self, *after):
        half, width = self.strip.shape[0] // 2, self.strip.shape[1]
        top, low = run(halves_kernel, (shaped(half, width),) * 2, None, (self.left, self.right), after=after)
        self.far_top, self.far_low = send_along(top, True, 1), send_along(low, True, -1)
        return low

    def swap_near(self):
        self.their_near = send_to(self.right, "c", 1), send_to(self.left, "c", 1)

    def gather_core(self):
        self.their_far = send_to(self.far_top, "c", 1), send_to(self.far_low, "c", 1)

    def pieces(self):
        mine = (self.strip, self.right, self.left, self.far_top, self.far_low)
        return mine + (self.their_strip,) + self.their_near + self.their_far


def each_piece(pieces, big, small, rows):
    own, right, left, far_top, far_low = pieces
    for turn, source, start, count in ((0, own, 0, 4), (1, right, 0, 4), (3, left, 0, 4), (2, far_top, 0, 2), (2, far_low, 2, 2)):
        for j in range(count):
            yield source, j * rows, (big + turn) & 3, (small + start + j) & 3


def unpack(target, rows, column, source, start, count, blocks):
    for block in range(blocks):
        at = column + block * LANES
        at = slice(at, at + LANES) if isinstance(at, int) else pl.ds(pl.multiple_of(at, LANES), LANES)
        target[rows, at] = source[start + block * count : start + (block + 1) * count, :]


def early_out_kernel(place, *refs):
    pieces, (down, up) = refs[:10], refs[10:]
    core, big, small = place[0], place[1], place[2]
    for side, half, along, across in ((pieces[:5], core, big, small), (pieces[5:], 1 - core, small, big)):
        for source, first, at_big, at_small in each_piece(side, along, across, EARLY_ROWS):
            unpack(down.at[half], rows_at(at_big, at_small, PIECE), 0, source, first, PIECE, 6)
            unpack(up, rows_at(at_big, at_small, PIECE // 2), half * DIM, source, first + 6 * PIECE, PIECE // 2, 6)


def late_out_kernel(place, up_early, *refs):
    pieces, (up, out_wo, qw, kw, vw, vec, biases, tiles) = refs[:10], refs[10:]
    core, big, small = place[0], place[1], place[2]
    count = PIECE // 2
    up[:HALF, :] = up_early[...]
    for side, half, along, across in ((pieces[:5], core, big, small), (pieces[5:], 1 - core, small, big)):
        for source, first, at_big, at_small in each_piece(side, along, across, LATE_ROWS):
            row = at_big * (4 * count) + at_small * count
            rows = pl.ds(pl.multiple_of(HALF + row, count), count)
            unpack(up, rows, half * DIM, source, first, count, 6)
            unpack(out_wo, rows_at(at_big, at_small, count), half * HALF, source, first + 6 * count, count, 3)
            rows = pl.ds(pl.multiple_of(half * HALF + row, count), count)
            for number, out in enumerate((qw, kw, vw)):
                unpack(out, rows, 0, source, first + (9 + 3 * number) * count, count, 3)
            tiles[half, at_big * 4 + at_small] = source[first + LATE_ROWS - 8 : first + LATE_ROWS, :]
    for block in range(DIM // LANES):
        vec[:, block * LANES : (block + 1) * LANES] = tiles[0, block]
    biases[...] = tiles[0, 6]


def on_device(
    tokens,
    seg_ids,
    pad_mask,
    query_weight,
    query_bias,
    key_weight,
    value_weight,
    value_bias,
    out_weight,
    out_bias,
    first_gain,
    first_shift,
    up_weight,
    up_bias,
    down_weight,
    down_bias,
    second_gain,
    second_shift,
    cotangent,
):
    tok = tokens.reshape(LEN, DIM)
    cot = cotangent.reshape(LEN, DIM)
    at_x, at_z, at_c = (lax.axis_index(name) for name in ("x", "z", "c"))
    at_big, at_small = jnp.where(at_c == 0, at_x, at_z), jnp.where(at_c == 0, at_z, at_x)
    place = jnp.stack([at_c, at_big, at_small]).astype(jnp.int32)
    row = lambda vector: vector.reshape(1, -1)
    ob, g1, s1, db, g2, s2 = (row(v) for v in (out_bias, first_gain, first_shift, down_bias, second_gain, second_shift))
    mat = lambda *shape: pltpu.VMEM(shape, F32)
    low_mat = lambda *shape: pltpu.VMEM(shape, LOW)

    first = (at_big * 4 + at_small) * PIECE
    up_shard = lax.dynamic_slice(up_weight, (first, at_c * DIM), (PIECE, DIM))
    down_shard = lax.dynamic_slice(down_weight, (at_c * DIM + first, 0), (PIECE, DIM))
    shard = lax.ppermute(jnp.concatenate([up_shard, down_shard]).astype(F32), ("w", "t"), CROSS)
    fetch = Group()
    q, k, v, att, lse, part, bias = run(
        attend_kernel,
        (shaped(LEN, HALF, kind=LOW),) * 4 + (shaped(LEN, 128), shaped(LEN + 8, DIM), shaped(LEN, LEN)),
        None,
        (tok, query_weight, key_weight, value_weight, out_weight, seg_ids, pad_mask, query_bias, value_bias, up_bias),
        [mat(LEN, LEN), low_mat(LEN, LEN), low_mat(LEN, DIM)]
        + [low_mat(DIM, HALF)] * 3
        + [low_mat(HALF, DIM), pltpu.VMEM((1, LEN), jnp.int32), pltpu.VMEM((1, LEN), jnp.int32)]
        + [mat(HALF), mat(HALF), mat(2 * DIM), pltpu.SemaphoreType.DMA((10,))],
        far=10,
    )
    part_other = send_to(part, "t", 1)
    part, shard = tie(part, shard)
    fetch.fan_out(shard)
    fetch.gather_near()
    fetch.gather_far()
    fetch.swap_near()
    fetch.gather_core()
    low, zhat1, r1, act_own, act_oth, dg_own, dg_oth, wup_oth = run(
        up_kernel,
        (
            shaped(LEN, DIM, kind=LOW),
            shaped(LEN, DIM),
            shaped(LEN, 1),
            shaped(LEN, 2 * DIM, kind=LOW),
            shaped(LEN, 2 * DIM, kind=LOW),
            shaped(LEN, 2 * DIM),
            shaped(LEN, 2 * DIM),
            shaped(2, DIM, DIM, kind=LOW),
        ),
        place,
        (part, part_other, tok, ob, g1, s1, up_weight) + fetch.pieces(),
        [mat(LEN, 256), mat(8, 2 * DIM)],
    )
    mixed, sgrad, slow, vec2, wdown_oth = run(
        down_kernel,
        (shaped(LEN, DIM, kind=LOW), shaped(LEN, DIM), shaped(LEN, DIM, kind=LOW), shaped(8, DIM), shaped(2, DIM, DIM, kind=LOW)),
        place,
        (zhat1, g1, s1, act_own, act_oth, down_weight, db, g2, s2, cot) + fetch.pieces(),
        [mat(LEN, DIM), mat(LEN, DIM), mat(3, 8, DIM)],
    )
    ug_own, vec3 = run(
        unit_kernel,
        (shaped(LEN, 2 * DIM, kind=LOW), shaped(8, DIM)),
        None,
        (slow, down_weight, dg_own),
        [mat(LEN, DIM), mat(2, 8, DIM)],
    )
    keep, send = run(
        early_grad_kernel,
        (shaped(16 * EARLY_ROWS, LANES),) * 2,
        place,
        (act_own, slow, low, ug_own),
        [mat(2, DIM, DIM), mat(2, HALF, DIM)],
    )
    early = Group(keep, send)
    after = early.core()
    first_grad, attg, gwo, vec = run(
        entry_kernel,
        (shaped(LEN, DIM), shaped(LEN, HALF, kind=LOW), shaped(HALF, DIM), shaped(8, DIM)),
        None,
        (slow, wdown_oth, dg_oth, up_weight, wup_oth, ug_own, sgrad, zhat1, r1, g1, att, out_weight, vec2, vec3),
        [mat(LEN, DIM), low_mat(LEN, DIM), mat(LEN, DIM), mat(LEN, DIM), low_mat(LEN, DIM), mat(3, 8, DIM)],
        after=after,
    )
    after = early.far(vec)
    dq, dk, dv = run(
        attend_back_kernel,
        (shaped(LEN, HALF, kind=LOW),) * 3,
        None,
        (bias, q, k, v, attg, lse),
        [mat(LEN, LEN), mat(LEN, LEN), low_mat(LEN, LEN), low_mat(LEN, LEN), mat(128, LEN), mat(128, LEN)],
        after=after,
    )
    after = early.near(dq)
    keep, send = run(
        late_grad_kernel,
        (shaped(16 * LATE_ROWS, LANES),) * 2,
        place,
        (tok, dq, dk, dv, low, ug_own, gwo, vec),
        [mat(2, HALF, DIM), mat(2, HALF, HALF), mat(2, HALF, 3 * HALF), mat(2, 16, 8, LANES)],
        after=after,
    )
    late = Group(keep, send)
    late.core()
    upper, lower = run(
        entry_part_kernel, (shaped(LEN // 2, DIM),) * 2, None, (dq, dk, dv, query_weight, key_weight, value_weight), after=keep
    )
    their_upper = send_to(upper, "t", 1)
    early.near_parts, late.other = tie(early.near_parts, late.other)
    early.direct()
    late.far()
    early.strips, late.far_parts, their_upper = tie(early.strips, late.far_parts, their_upper)
    early.pair()
    late.near()
    early.twin, late.near_parts = tie(early.twin, late.near_parts)
    early.gather_small()
    late.direct()
    early.parts, late.strips = tie(early.parts, late.strips)
    early.gather_near()
    late.pair()
    early.right, early.left, early.their_strip, late.twin = tie(early.right, early.left, early.their_strip, late.twin)
    early.gather_far()
    late.gather_small()
    early.right, early.left, early.far_top, early.far_low, late.parts, lower = tie(
        early.right, early.left, early.far_top, early.far_low, late.parts, lower
    )
    their_lower = send_to(lower, "t", 1)
    early.swap_near()
    early.gather_core()
    late.gather_near()
    down_sum, up_early = run(early_out_kernel, (shaped(2, DIM, DIM), shaped(HALF, 2 * DIM)), place, early.pieces(), spare=14)
    late.right, late.left, late.their_strip, up_early = tie(late.right, late.left, late.their_strip, up_early)
    late.gather_far()
    late.swap_near()
    late.far_top, late.far_low, their_lower = tie(late.far_top, late.far_low, their_lower)
    input_gradient = run(total_kernel, shaped(LEN, DIM), None, (first_grad, upper, lower, their_upper, their_lower))
    late.gather_core()
    weight = shaped(DIM, HALF)
    up_sum, ow, qw, kw, vw, vec, biases = run(
        late_out_kernel,
        (shaped(DIM, 2 * DIM), shaped(HALF, DIM), weight, weight, weight, shaped(8, DIM), shaped(8, LANES)),
        place,
        (up_early,) + late.pieces(),
        [mat(2, 16, 8, LANES)],
        spare=18,
    )
    db, sg, ss, ob, fg, fs = (vec[j] for j in range(6))
    return (
        mixed.reshape(1, LEN, DIM),
        input_gradient.reshape(1, LEN, DIM),
        qw,
        biases[0:3].reshape(HALF),
        kw,
        vw,
        biases[3:6].reshape(HALF),
        ow,
        ob,
        fg,
        fs,
        up_sum,
        vec[6:8].reshape(2 * DIM),
        down_sum.reshape(2 * DIM, DIM),
        db,
        sg,
        ss,
    )


ROWS_AXES = ("x", "w", "z", "c")


def solution(mesh):
    fine = jax.sharding.Mesh(mesh.devices.reshape(4, 2, 4, 2, 2), ROWS_AXES + ("t",))
    by_row, ids = P(ROWS_AXES, None, None), P(ROWS_AXES, None)
    columns, units, rows, whole = P(None, "t"), P("t"), P("t", None), P()
    return jax.shard_map(
        on_device,
        mesh=fine,
        in_specs=(
            (by_row, ids, ids, columns, units, columns, columns, units, rows)
            + (whole, whole, whole, columns, units, rows, whole, whole, whole, by_row)
        ),
        out_specs=(
            (by_row, by_row, columns, units, columns, columns, units, rows)
            + (whole, whole, whole, columns, units, rows, whole, whole, whole)
        ),
        check_vma=False,
    )
```
